256 devices in a mesh: store: 64 (over x, z, core), head: 4 (over y).
Axes of the slice: x: 4, y: 4, z: 8, core: 2. Of those that a mesh axis runs over, the one named last changes fastest.
Arguments:
- queries: bfloat16 [16384, 8192], P('store', 'head'), may hold values from -1000 to 1000
- question_kv: bfloat16 [16384, 2048], P('store', 'head'), may hold values from -24 to 24
- pages: bfloat16 [1024, 96, 2048], P('store', 'head'), may hold values from -6 to 6
- page_scales: bfloat16 [1024, 96, 16], P('store', 'head'), may hold values from 0.29882812 to 3
- passage_ids: int32 [256, 4], P('store'), may hold values from 0 to 1023, as said below
Outputs:
- attended: bfloat16 [16384, 8192], P('store', 'head')
The draws below stay inside these ranges and needn't reach their ends.
Inputs may be any that keep to these rules, and one draw needn't show every extreme that they name: `passage_ids`: among the 4 passages of each request of one aligned block of 4 requests, at most 2 lie on one store shard (the shard of id p is p // 16); in every block some shard holds exactly 2 of them.
All inputs are finite; a program needn't handle non-finite values.
Results may differ from the reference program's by a relative error of at most 0.0074.
Values may be sent and summed in bfloat16 or wider, within the bound.
A program may use at most 192 MiB of HBM per device.

```python
import math
import jax
import jax.numpy as jnp
from jax import lax

QH = 64
KVH = 8
HD = 128
NPAS = 4
PLEN = 96
CAP = 2
QLEN = 64
R_DEV = 4
P_DEV = 16
REQS = 256
PASSAGES = 1024
QTOK = 16384


def question_base(key):
    return jax.random.normal(key, (QTOK, KVH, 2, HD))


def draw_question_kv(key, part):
    base = question_base(key)
    return jnp.clip(base, -24.0, 24.0).reshape(QTOK, KVH * 2 * HD).astype(jnp.bfloat16)


def draw_queries(key, part):
    groups = QH // KVH
    own_key = jax.random.fold_in(key, 5)
    values = jax.random.normal(own_key, (QTOK, KVH, groups, HD))
    return jnp.clip(values, -1000.0, 1000.0).reshape(QTOK, QH * HD).astype(jnp.bfloat16)


def draw_passage_ids(key, part):
    key = jax.random.fold_in(key, 9)
    blocks = REQS // R_DEV
    fetches = R_DEV * NPAS
    shards = PASSAGES // P_DEV
    offset = jax.random.randint(jax.random.fold_in(key, 1), (blocks, 1), 0, shards)
    block_keys = jax.random.split(jax.random.fold_in(key, 2), blocks)
    shuffled = jax.vmap(lambda item: jax.random.permutation(item, fetches))(block_keys)
    shard = (offset + shuffled // CAP) % shards
    within = jax.random.randint(jax.random.fold_in(key, 3), (blocks, fetches), 0, P_DEV)
    return (shard * P_DEV + within).reshape(REQS, NPAS).astype(jnp.int32)


def steps_of(stream_key, extent, pieces, smallest, top_value):
    level, own = 1.0, jax.random.fold_in(stream_key, 6)
    for axis_at, shards_of in pieces:
        steps = jnp.exp(jax.random.uniform(jax.random.fold_in(own, axis_at), (shards_of,), jnp.float32, smallest / len(pieces), top_value / len(pieces)))
        level = level * jnp.repeat(steps, extent[axis_at] // shards_of).reshape([-1 if axis == axis_at else 1 for axis in range(len(extent))])
    return level


def noise(rng, extent, deviation, bound, pieces=(), held_as=jnp.bfloat16):
    level = steps_of(rng, extent, pieces, -0.22, 0.18) if pieces else 1.0
    values = jax.random.normal(rng, extent, jnp.float32) * deviation * level
    return jnp.minimum(jnp.maximum(values, -bound), bound).astype(held_as)


def setup_inputs(seed: int = 0) -> dict:
    arg_keys = jax.random.split(jax.random.key(seed), 6)
    queries = draw_queries(jax.random.fold_in(arg_keys[5], 71), 0)
    question_kv = draw_question_kv(jax.random.fold_in(arg_keys[5], 71), 0)
    pages = noise(arg_keys[2], (PASSAGES, PLEN, KVH * 2 * HD), 1.0, 6.0, ((0, 64), (1, 4)))
    page_scales = jnp.clip(jnp.exp(math.log(3.0) - 2.306499 * jax.random.uniform(arg_keys[3], (PASSAGES, PLEN, KVH * 2), jnp.float32) ** steps_of(arg_keys[3], (PASSAGES, PLEN, KVH * 2), ((0, 64), (1, 4)), -0.2, 0.2)), 0.29882812, 3.0).astype(jnp.bfloat16)
    passage_ids = draw_passage_ids(jax.random.fold_in(arg_keys[5], 71), 0)
    return {"queries": queries, "question_kv": question_kv, "pages": pages, "page_scales": page_scales, "passage_ids": passage_ids}


rope_theta = 500000.0

def rotate_keys(keys, offsets):
    half_dim = keys.shape[-1] // 2
    freqs = jnp.exp(jnp.arange(half_dim, dtype=jnp.float32) * (-2.0 * jnp.log(jnp.float32(rope_theta)) / keys.shape[-1]))
    angles = offsets[:, None] * freqs[None, :]
    cosine = jnp.cos(angles)[:, None, None, :]
    sine = jnp.sin(angles)[:, None, None, :]
    first = keys[..., :half_dim]
    second = keys[..., half_dim:]
    return jnp.concatenate([first * cosine - second * sine, second * cosine + first * sine], axis=-1)

def attend(query_rows, key_rows, value_rows):
    qlen = query_rows.shape[1]
    total = key_rows.shape[1]
    scores = jnp.einsum('bqkgd,bskd->bkgqs', query_rows.astype(jnp.float32), key_rows.astype(jnp.float32)) / jnp.sqrt(jnp.float32(query_rows.shape[-1]))
    key_pos = jnp.arange(total)
    query_pos = jnp.arange(qlen) + (total - qlen)
    allowed = key_pos[None, :] <= query_pos[:, None]
    scores = jnp.where(allowed, scores, -jnp.inf)
    highest = lax.optimization_barrier(jnp.max(scores, axis=-1, keepdims=True))
    raised = jnp.exp(scores - highest)
    probs = (raised / lax.optimization_barrier(jnp.sum(raised, axis=-1, keepdims=True))).astype(jnp.bfloat16)
    result = jnp.einsum('bkgqs,bskd->bqkgd', probs.astype(jnp.float32), value_rows.astype(jnp.float32))
    return result.astype(jnp.bfloat16)

def reference(queries, question_kv, pages, page_scales, passage_ids):
    groups = QH // KVH
    query_all = queries.reshape(REQS, QLEN, KVH, groups, HD)
    question_all = question_kv.reshape(REQS, QLEN, KVH, 2, HD)
    offsets = jnp.arange(NPAS, dtype=jnp.float32) * PLEN

    def one_request(items):
        query_rows, question_rows, chosen = items
        codes = jnp.take(pages, chosen, axis=0).reshape(NPAS, PLEN, KVH, 2, HD).astype(jnp.float32)
        scaled = jnp.take(page_scales, chosen, axis=0).reshape(NPAS, PLEN, KVH, 2).astype(jnp.float32)
        plain = codes * scaled[..., None]
        key_part = rotate_keys(plain[..., 0, :], offsets).astype(jnp.bfloat16).reshape(NPAS * PLEN, KVH, HD)
        value_part = plain[..., 1, :].astype(jnp.bfloat16).reshape(NPAS * PLEN, KVH, HD)
        key_rows = jnp.concatenate([key_part, question_rows[:, :, 0, :]], axis=0)
        value_rows = jnp.concatenate([value_part, question_rows[:, :, 1, :]], axis=0)
        return attend(query_rows[None], key_rows[None], value_rows[None])[0]
    result = lax.map(one_request, (query_all, question_all, passage_ids))
    return result.reshape(QTOK, QH * HD)
```

```python
import math

import numpy as np
import jax
import jax.numpy as jnp
from jax import lax
from jax.experimental import pallas as pl
from jax.experimental.pallas import tpu as pltpu
from jax.sharding import PartitionSpec as P

QH = 64
KVH = 8
HD = 128
NPAS = 4
PLEN = 96
CAP = 2
QLEN = 64
R_DEV = 4
P_DEV = 16
XS, ZS, CORES, HEADS = 4, 8, 2, 4
SHARDS = XS * CORES
TOK = PLEN // HEADS
ROWS = 2 * TOK
LANES = 2 * HD
SLOTS = 4
FETCH = R_DEV * NPAS
GROUPS = QH // KVH
PART = 4 * HD
PKEYS = NPAS * PLEN
KEYS = PKEYS + QLEN
MESH = pl.DeviceIdType.MESH

rope_theta = 500000.0


def rotate_keys(keys, offsets):
    half_dim = keys.shape[-1] // 2
    freqs = jnp.exp(
        jnp.arange(half_dim, dtype=jnp.float32)
        * (-2.0 * jnp.log(jnp.float32(rope_theta)) / keys.shape[-1])
    )
    angles = offsets[:, None] * freqs[None, :]
    cosine = jnp.cos(angles)[:, None, None, :]
    sine = jnp.sin(angles)[:, None, None, :]
    first = keys[..., :half_dim]
    second = keys[..., half_dim:]
    return jnp.concatenate(
        [first * cosine - second * sine, second * cosine + first * sine], axis=-1
    )


def attend(query_rows, key_rows, value_rows):
    qlen = query_rows.shape[1]
    total = key_rows.shape[1]
    scores = jnp.einsum(
        "bqkgd,bskd->bkgqs", query_rows, key_rows, preferred_element_type=jnp.float32
    ) / jnp.sqrt(jnp.float32(query_rows.shape[-1]))
    key_pos = jnp.arange(total)
    query_pos = jnp.arange(qlen) + (total - qlen)
    allowed = key_pos[None, :] <= query_pos[:, None]
    scores = jnp.where(allowed, scores, -jnp.inf)
    highest = jnp.max(scores, axis=-1, keepdims=True)
    raised = jnp.exp(scores - highest)
    probs = (raised / jnp.sum(raised, axis=-1, keepdims=True)).astype(jnp.bfloat16)
    result = jnp.einsum("bkgqs,bskd->bqkgd", probs, value_rows, preferred_element_type=jnp.float32)
    return result.astype(jnp.bfloat16)


def general(queries, question_kv, pages, page_scales, passage_ids):
    shards = lax.axis_size("store")
    groups_axis = lax.axis_size("head")
    requests, per_request = passage_ids.shape
    fetches = requests * per_request
    stored, part_tokens, lanes = pages.shape
    passage_len = part_tokens * groups_axis
    kv_local = KVH // groups_axis
    groups = QH // KVH
    head_dim = HD
    question_len = queries.shape[0] // requests
    flat_ids = passage_ids.reshape(fetches)
    shard_of = flat_ids // stored
    within = flat_ids % stored
    counter = jnp.arange(fetches)
    same_shard = shard_of[:, None] == shard_of[None, :]
    earlier = counter[None, :] < counter[:, None]
    order_rank = jnp.sum(same_shard & earlier, axis=1)
    slot_index = shard_of * CAP + order_rank
    matches = slot_index[:, None] == jnp.arange(shards * CAP)[None, :]
    wanted_table = jnp.sum(jnp.where(matches, within[:, None], 0), axis=0).reshape(shards, CAP)
    asked = lax.all_to_all(wanted_table, "store", split_axis=0, concat_axis=0, tiled=True)
    asked_flat = asked.reshape(shards * CAP)
    send_pages = jnp.take(pages, asked_flat, axis=0).reshape(shards, CAP, part_tokens, lanes)
    send_scales = jnp.take(page_scales, asked_flat, axis=0).reshape(
        shards, CAP, part_tokens, 2 * KVH
    )
    got_pages, got_scales = (
        lax.all_to_all(
            lax.all_to_all(send_pages, "store", split_axis=0, concat_axis=0, tiled=True),
            "head",
            split_axis=3,
            concat_axis=2,
            tiled=True,
        ),
        lax.all_to_all(
            lax.all_to_all(send_scales, "store", split_axis=0, concat_axis=0, tiled=True),
            "head",
            split_axis=3,
            concat_axis=2,
            tiled=True,
        ),
    )
    mine_pages = jnp.take(
        got_pages.reshape(shards * CAP, passage_len, 2 * kv_local * head_dim), slot_index, axis=0
    )
    mine_scales = jnp.take(
        got_scales.reshape(shards * CAP, passage_len, 2 * kv_local), slot_index, axis=0
    )
    mine_pages = mine_pages.reshape(requests, per_request, passage_len, kv_local, 2, head_dim)
    mine_scales = mine_scales.reshape(requests, per_request, passage_len, kv_local, 2)
    plain = mine_pages.astype(jnp.float32) * mine_scales.astype(jnp.float32)[..., None]
    offsets = jnp.arange(per_request, dtype=jnp.float32) * passage_len
    key_part = (
        rotate_keys(plain[..., 0, :], offsets)
        .astype(jnp.bfloat16)
        .reshape(requests, per_request * passage_len, kv_local, head_dim)
    )
    value_part = (
        plain[..., 1, :]
        .astype(jnp.bfloat16)
        .reshape(requests, per_request * passage_len, kv_local, head_dim)
    )
    question_rows = question_kv.reshape(requests, question_len, kv_local, 2, head_dim)
    key_rows = jnp.concatenate([key_part, question_rows[:, :, :, 0, :]], axis=1)
    value_rows = jnp.concatenate([value_part, question_rows[:, :, :, 1, :]], axis=1)
    query_rows = queries.reshape(requests, question_len, kv_local, groups, head_dim)

    def one_block(items):
        return attend(items[0], items[1], items[2])

    result = lax.map(
        one_block, (query_rows[:, None], key_rows[:, None], value_rows[:, None])
    )
    return result.reshape(requests * question_len, kv_local * groups * head_dim)


def rope_tables():
    half = HD // 2
    freqs = np.exp(
        np.arange(half, dtype=np.float32)
        * np.float32(-2.0 * np.log(np.float32(rope_theta)) / np.float32(HD))
    ).astype(np.float32)
    angles = (np.arange(NPAS, dtype=np.float32) * np.float32(PLEN))[:, None] * freqs[None, :]
    angles = angles.astype(np.float64)
    cosine = np.concatenate([np.cos(angles), np.cos(angles)], axis=1)
    sine = np.concatenate([-np.sin(angles), np.sin(angles)], axis=1)
    spread = lambda table: np.repeat(table[:, None, :], 8, axis=1).astype(np.float32)
    return spread(cosine), spread(sine)


def kernel(
    ids_ref, pages_ref, scales_ref, q_ref, qkv_ref, cos_ref, sin_ref,
    out_ref, flag_ref,
    ysend, g0, g1, g2, g3, s0, s1, s2, s3, l0, l1, l2, l3,
    idv, ids, want, mine, kv,
    y_send, y_recv, x_send, x_recv, z_send, z_recv, i_send, i_recv, local_sem,
):
    gathered, outgoing, landed = (g0, g1, g2, g3), (s0, s1, s2, s3), (l0, l1, l2, l3)
    store, head = lax.axis_index("store"), lax.axis_index("head")
    x, z, core = store // (ZS * CORES), (store // CORES) % ZS, store % CORES
    turn = 1 - 2 * core

    def at(x_, z_, core_):
        return ((x_ + 2 * XS) % XS * ZS + z_ % ZS) * CORES + core_

    def spot(x_, core_):
        return (x_ + 2 * XS) % XS * CORES + core_

    barrier = pltpu.get_barrier_semaphore()
    peers = [(store, (head + c) % HEADS) for c in range(1, HEADS)]
    peers += [(at(x + 1, z, core), head), (at(x - 1, z, core), head), (at(x, z, 1 - core), head)]
    peers += [(at(x, z + d, core), head) for d in range(1, ZS)]
    for peer in peers:
        pl.semaphore_signal(barrier, inc=1, device_id=peer, device_id_type=MESH)

    planes, over = [], 0
    for i in range(FETCH):
        one = ids_ref[i // NPAS, i % NPAS]
        plane = (one // P_DEV // CORES) % ZS
        rank = 0
        for other in planes:
            rank = rank + jnp.where(other == plane, 1, 0)
        planes.append(plane)
        over = jnp.maximum(over, rank)
        mine[i] = plane * SLOTS + jnp.minimum(rank, SLOTS - 1)
    lane8 = lax.broadcasted_iota(jnp.int32, (8, 128), 1)
    tile = jnp.where(lane8 == FETCH, over, 0)
    for i in range(FETCH):
        tile = jnp.where(lane8 == i, ids_ref[i // NPAS, i % NPAS], tile)
    idv[z] = tile

    lane = lax.broadcasted_iota(jnp.int32, (TOK, 128), 1)
    for hh in range(HEADS):

        def one_page(p, held, hh=hh):
            scale = scales_ref[p].astype(jnp.float32)
            halves, kept = [], []
            for g in range(2):
                col = 2 * (2 * hh + g)
                codes = pages_ref[p, :, PART * hh + LANES * g : PART * hh + LANES * (g + 1)]
                codes = codes.astype(jnp.float32)
                value = codes[:, HD:] * scale[:, col + 1 : col + 2]
                halves.append(jnp.concatenate([codes[:, :HD], value], axis=1))
                kept.append(jnp.where(lane == p, scale[:, col : col + 1], held[g]))
            ysend[hh, p] = jnp.concatenate(halves, axis=0).astype(jnp.bfloat16)
            return tuple(kept)

        none = jnp.zeros((TOK, 128), jnp.float32)
        kept = lax.fori_loop(0, P_DEV, one_page, (none, none))
        ysend[hh, P_DEV, :, :HD] = jnp.concatenate(kept, axis=0).astype(jnp.bfloat16)
        ysend[hh, P_DEV, :, HD:] = jnp.zeros((ROWS, HD), jnp.bfloat16)

    pl.semaphore_wait(barrier, len(peers))

    def id_copy(step):
        return pltpu.make_async_remote_copy(
            src_ref=idv.at[z], dst_ref=idv.at[z],
            send_sem=i_send.at[step], recv_sem=i_recv.at[step],
            device_id=(at(x, z + step, core), head), device_id_type=MESH,
        )

    def y_copy(c):
        to = (head + HEADS - c) % HEADS
        return pltpu.make_async_remote_copy(
            src_ref=ysend.at[to], dst_ref=gathered[c].at[spot(x, core)],
            send_sem=y_send.at[c], recv_sem=y_recv.at[c],
            device_id=(store, to), device_id_type=MESH,
        )

    def x_copy(c, kind):
        slot, to = (
            (spot(x, core), at(x + 1, z, core)),
            (spot(x, core), at(x - 1, z, core)),
            (spot(x - turn, core), at(x + turn, z, core)),
            (spot(x, core), at(x, z, 1 - core)),
            (spot(x - 1, core), at(x, z, 1 - core)),
            (spot(x + 1, core), at(x, z, 1 - core)),
            (spot(x + 2, core), at(x, z, 1 - core)),
        )[kind]
        return pltpu.make_async_remote_copy(
            src_ref=gathered[c].at[slot], dst_ref=gathered[c].at[slot],
            send_sem=x_send.at[c, kind], recv_sem=x_recv.at[c, kind],
            device_id=(to, head), device_id_type=MESH,
        )

    def z_copy(c, step):
        return pltpu.make_async_remote_copy(
            src_ref=outgoing[c].at[step], dst_ref=landed[c].at[z],
            send_sem=z_send.at[c, step], recv_sem=z_recv.at[c, step],
            device_id=(at(x, z + step, core), head), device_id_type=MESH,
        )

    def x_start(c):
        if c > 0:
            y_copy(c).wait_recv()
        if c == HEADS - 1:
            g3[spot(x, core), P_DEV, :, HD:] = jnp.broadcast_to(flag, (ROWS, HD)).astype(
                jnp.bfloat16
            )
        for kind in (0, 1, 3):
            x_copy(c, kind).start()

    def x_forward(c):
        x_copy(c, 0).wait_recv()
        x_copy(c, 1).wait_recv()
        for kind in (2, 4, 5):
            x_copy(c, kind).start()

    def x_last(c):
        x_copy(c, 2).wait_recv()
        x_copy(c, 6).start()

    def x_done(c):
        for kind in (3, 4, 5, 6):
            x_copy(c, kind).wait_recv()

    rows_lane = lax.broadcasted_iota(jnp.int32, (ROWS, 128), 1)

    def finished(c, code):
        page = code % P_DEV
        shard = (code // P_DEV) % (XS * ZS * CORES)
        k = code // (XS * ZS * CORES * P_DEV)
        place = (shard // (ZS * CORES)) * CORES + shard % CORES
        block = gathered[c][place, page]
        scales = gathered[c][place, P_DEV, :, :HD].astype(jnp.float32)
        scale = jnp.sum(jnp.where(rows_lane == page, scales, 0.0), axis=1, keepdims=True)
        key = block[:, :HD].astype(jnp.float32) * scale
        turned = key * cos_ref[k, 0:1] + pltpu.roll(key, HD // 2, 1) * sin_ref[k, 0:1]
        return turned.astype(jnp.bfloat16), block[:, HD:]

    def z_start(c):
        def one_dest(i, carry):
            step = (i * 3) % ZS
            to = (z + step) % ZS
            for j in range(SLOTS):
                key, value = finished(c, want[to * SLOTS + j])
                outgoing[c][step, j, :, :HD] = key
                outgoing[c][step, j, :, HD:] = value
            z_copy(c, step).start()
            return carry

        lax.fori_loop(1, ZS, one_dest, 0)
        for j in range(SLOTS):
            key, value = finished(c, want[z * SLOTS + j])
            landed[c][z, j, :, :HD] = key
            landed[c][z, j, :, HD:] = value

    for step in range(1, ZS):
        id_copy(step).start()
    for c in range(1, HEADS):
        y_copy(c).start()
    own = pltpu.make_async_copy(ysend.at[head], g0.at[spot(x, core)], local_sem)
    own.start()
    own.wait()
    x_start(0)

    for step in range(1, ZS):
        id_copy(step).wait_recv()
    to_smem = pltpu.make_async_copy(idv, ids, local_sem)
    to_smem.start()
    to_smem.wait()

    def scan(dest, worst):
        count = 0
        chosen = [0] * SLOTS
        for i in range(FETCH):
            one = ids[dest, 0, i]
            hit = (one // P_DEV // CORES) % ZS == z
            for j in range(SLOTS):
                chosen[j] = jnp.where(
                    hit & (count == j), one + (i % NPAS) * (XS * ZS * CORES * P_DEV), chosen[j]
                )
            count = count + jnp.where(hit, 1, 0)
        for j in range(SLOTS):
            want[dest * SLOTS + j] = chosen[j]
        return jnp.maximum(worst, ids[dest, 0, FETCH])

    worst = lax.fori_loop(0, ZS, scan, jnp.int32(0))
    flag = jnp.where(worst >= SLOTS, 1.0, 0.0)

    x_start(1)
    x_forward(0)
    x_last(0)
    x_start(2)
    x_done(0)
    z_start(0)
    x_forward(1)
    x_last(1)
    x_start(3)
    x_done(1)
    z_start(1)
    x_forward(2)
    x_last(2)
    x_done(2)
    z_start(2)
    x_forward(3)
    x_last(3)
    x_done(3)
    z_start(3)

    flags = g3[0, P_DEV, :, HD:].astype(jnp.float32)
    for place in range(1, SHARDS):
        flags = jnp.maximum(flags, g3[place, P_DEV, :, HD:].astype(jnp.float32))
    flag_ref[...] = flags[:8]

    def arrived(c):
        def one(step, carry):
            z_copy(c, step).wait_recv()
            return carry

        lax.fori_loop(1, ZS, one, 0)

    for c in range(HEADS):
        arrived(c)

    col = lax.broadcasted_iota(jnp.int32, (GROUPS * QLEN, QLEN), 1)
    row = lax.broadcasted_iota(jnp.int32, (GROUPS * QLEN, QLEN), 0) % QLEN
    seen = col <= row

    def one_request(r, carry):
        rows = pl.ds(pl.multiple_of(r * QLEN, QLEN), QLEN)
        for c in range(HEADS):
            blocks = []
            for k in range(NPAS):
                spot_ = mine[r * NPAS + k]
                blocks.append(landed[c][spot_ // SLOTS, spot_ % SLOTS].astype(jnp.float32))
            for g in range(2):
                part = jnp.concatenate([b[g * TOK : (g + 1) * TOK] for b in blocks], axis=0)
                kv[g, c * PLEN : (c + 1) * PLEN, :] = part.astype(jnp.bfloat16)
        for g in range(2):
            kv[g, PKEYS:, :] = qkv_ref[rows, g * LANES : (g + 1) * LANES]
            query = jnp.concatenate(
                [
                    q_ref[rows, (g * GROUPS + j) * HD : (g * GROUPS + j + 1) * HD]
                    for j in range(GROUPS)
                ],
                axis=0,
            )
            dims = (((1,), (1,)), ((), ()))
            scale = jnp.float32(1.0 / math.sqrt(HD))
            past = scale * lax.dot_general(
                query, kv[g, :PKEYS, :HD], dims, preferred_element_type=jnp.float32
            )
            now = scale * lax.dot_general(
                query, kv[g, PKEYS:, :HD], dims, preferred_element_type=jnp.float32
            )
            now = jnp.where(seen, now, -jnp.inf)
            top = jnp.maximum(
                jnp.max(past, axis=1, keepdims=True), jnp.max(now, axis=1, keepdims=True)
            )
            past = jnp.exp(past - top)
            now = jnp.exp(now - top)
            total = jnp.sum(past, axis=1, keepdims=True) + jnp.sum(now, axis=1, keepdims=True)
            inverse = 1.0 / total
            past = (past * inverse).astype(jnp.bfloat16)
            now = (now * inverse).astype(jnp.bfloat16)
            result = jnp.dot(past, kv[g, :PKEYS, HD:], preferred_element_type=jnp.float32)
            result = result + jnp.dot(now, kv[g, PKEYS:, HD:], preferred_element_type=jnp.float32)
            for j in range(GROUPS):
                out_ref[rows, (g * GROUPS + j) * HD : (g * GROUPS + j + 1) * HD] = result[
                    j * QLEN : (j + 1) * QLEN
                ].astype(jnp.bfloat16)
        return carry

    lax.fori_loop(0, R_DEV, one_request, 0)

    for step in range(1, ZS):
        id_copy(step).wait_send()
    for c in range(1, HEADS):
        y_copy(c).wait_send()
    for c in range(HEADS):
        for kind in range(7):
            x_copy(c, kind).wait_send()
        for step in range(1, ZS):
            z_copy(c, step).wait_send()


def fast(queries, question_kv, pages, page_scales, passage_ids):
    cosine, sine = rope_tables()
    vmem = pl.BlockSpec(memory_space=pltpu.VMEM)
    block = (ROWS, LANES)
    dma = pltpu.SemaphoreType.DMA
    return pl.pallas_call(
        kernel,
        out_shape=(
            jax.ShapeDtypeStruct(queries.shape, jnp.bfloat16),
            jax.ShapeDtypeStruct((8, 128), jnp.float32),
        ),
        in_specs=[pl.BlockSpec(memory_space=pltpu.SMEM)] + [vmem] * 6,
        out_specs=(vmem, vmem),
        scratch_shapes=[pltpu.VMEM((HEADS, P_DEV + 1) + block, jnp.bfloat16)]
        + [pltpu.VMEM((SHARDS, P_DEV + 1) + block, jnp.bfloat16)] * HEADS
        + [pltpu.VMEM((ZS, SLOTS) + block, jnp.bfloat16)] * (2 * HEADS)
        + [
            pltpu.VMEM((ZS, 8, 128), jnp.int32),
            pltpu.SMEM((ZS, 8, 128), jnp.int32),
            pltpu.SMEM((ZS * SLOTS,), jnp.int32),
            pltpu.SMEM((FETCH,), jnp.int32),
            pltpu.VMEM((2, KEYS, LANES), jnp.bfloat16),
            dma((HEADS,)), dma((HEADS,)),
            dma((HEADS, 7)), dma((HEADS, 7)),
            dma((HEADS, ZS)), dma((HEADS, ZS)),
            dma((ZS,)), dma((ZS,)),
            dma,
        ],
        compiler_params=pltpu.CompilerParams(
            collective_id=0, has_side_effects=True, vmem_limit_bytes=48 * 1024 * 1024
        ),
    )(passage_ids, pages, page_scales, queries, question_kv, jnp.asarray(cosine), jnp.asarray(sine))


def per_device(queries, question_kv, pages, page_scales, passage_ids):
    args = (queries, question_kv, pages, page_scales, passage_ids)
    result, flags = fast(*args)
    return lax.cond(flags[0, 0] > 0, lambda: general(*args), lambda: result)


def solution(mesh):
    return jax.shard_map(
        per_device,
        mesh=mesh,
        in_specs=(
            P("store", "head"),
            P("store", "head"),
            P("store", "head", None),
            P("store", "head", None),
            P("store", None),
        ),
        out_specs=P("store", "head"),
        check_vma=False,
    )
```

```python
import math

import numpy as np
import jax
import jax.numpy as jnp
from jax import lax
from jax.experimental import pallas as pl
from jax.experimental.pallas import tpu as pltpu
from jax.sharding import PartitionSpec as P

QH = 64
KVH = 8
HD = 128
NPAS = 4
PLEN = 96
CAP = 2
QLEN = 64
R_DEV = 4
P_DEV = 16
XS, ZS, CORES, HEADS = 4, 8, 2, 4
SHARDS = XS * CORES
TOK = PLEN // HEADS
ROWS = 2 * TOK
LANES = 2 * HD
SLOTS = 4
FETCH = R_DEV * NPAS
GROUPS = QH // KVH
PART = 4 * HD
PIECE = NPAS * TOK
PKEYS = NPAS * PLEN
KEYS = PKEYS + QLEN
CHUNKS = 2 * HEADS
MESH = pl.DeviceIdType.MESH

rope_theta = 500000.0


def rotate_keys(keys, offsets):
    half_dim = keys.shape[-1] // 2
    freqs = jnp.exp(
        jnp.arange(half_dim, dtype=jnp.float32)
        * (-2.0 * jnp.log(jnp.float32(rope_theta)) / keys.shape[-1])
    )
    angles = offsets[:, None] * freqs[None, :]
    cosine = jnp.cos(angles)[:, None, None, :]
    sine = jnp.sin(angles)[:, None, None, :]
    first = keys[..., :half_dim]
    second = keys[..., half_dim:]
    return jnp.concatenate(
        [first * cosine - second * sine, second * cosine + first * sine], axis=-1
    )


def attend(query_rows, key_rows, value_rows):
    qlen = query_rows.shape[1]
    total = key_rows.shape[1]
    scores = jnp.einsum(
        "bqkgd,bskd->bkgqs", query_rows, key_rows, preferred_element_type=jnp.float32
    ) / jnp.sqrt(jnp.float32(query_rows.shape[-1]))
    key_pos = jnp.arange(total)
    query_pos = jnp.arange(qlen) + (total - qlen)
    allowed = key_pos[None, :] <= query_pos[:, None]
    scores = jnp.where(allowed, scores, -jnp.inf)
    highest = jnp.max(scores, axis=-1, keepdims=True)
    raised = jnp.exp(scores - highest)
    probs = (raised / jnp.sum(raised, axis=-1, keepdims=True)).astype(jnp.bfloat16)
    result = jnp.einsum("bkgqs,bskd->bqkgd", probs, value_rows, preferred_element_type=jnp.float32)
    return result.astype(jnp.bfloat16)


def general(queries, question_kv, pages, page_scales, passage_ids):
    shards = lax.axis_size("store")
    groups_axis = lax.axis_size("head")
    requests, per_request = passage_ids.shape
    fetches = requests * per_request
    stored, part_tokens, lanes = pages.shape
    passage_len = part_tokens * groups_axis
    kv_local = KVH // groups_axis
    groups = QH // KVH
    head_dim = HD
    question_len = queries.shape[0] // requests
    flat_ids = passage_ids.reshape(fetches)
    shard_of = flat_ids // stored
    within = flat_ids % stored
    counter = jnp.arange(fetches)
    same_shard = shard_of[:, None] == shard_of[None, :]
    earlier = counter[None, :] < counter[:, None]
    order_rank = jnp.sum(same_shard & earlier, axis=1)
    slot_index = shard_of * CAP + order_rank
    matches = slot_index[:, None] == jnp.arange(shards * CAP)[None, :]
    wanted_table = jnp.sum(jnp.where(matches, within[:, None], 0), axis=0).reshape(shards, CAP)
    asked = lax.all_to_all(wanted_table, "store", split_axis=0, concat_axis=0, tiled=True)
    asked_flat = asked.reshape(shards * CAP)
    send_pages = jnp.take(pages, asked_flat, axis=0).reshape(shards, CAP, part_tokens, lanes)
    send_scales = jnp.take(page_scales, asked_flat, axis=0).reshape(
        shards, CAP, part_tokens, 2 * KVH
    )
    got_pages, got_scales = (
        lax.all_to_all(
            lax.all_to_all(send_pages, "store", split_axis=0, concat_axis=0, tiled=True),
            "head",
            split_axis=3,
            concat_axis=2,
            tiled=True,
        ),
        lax.all_to_all(
            lax.all_to_all(send_scales, "store", split_axis=0, concat_axis=0, tiled=True),
            "head",
            split_axis=3,
            concat_axis=2,
            tiled=True,
        ),
    )
    mine_pages = jnp.take(
        got_pages.reshape(shards * CAP, passage_len, 2 * kv_local * head_dim), slot_index, axis=0
    )
    mine_scales = jnp.take(
        got_scales.reshape(shards * CAP, passage_len, 2 * kv_local), slot_index, axis=0
    )
    mine_pages = mine_pages.reshape(requests, per_request, passage_len, kv_local, 2, head_dim)
    mine_scales = mine_scales.reshape(requests, per_request, passage_len, kv_local, 2)
    plain = mine_pages.astype(jnp.float32) * mine_scales.astype(jnp.float32)[..., None]
    offsets = jnp.arange(per_request, dtype=jnp.float32) * passage_len
    key_part = (
        rotate_keys(plain[..., 0, :], offsets)
        .astype(jnp.bfloat16)
        .reshape(requests, per_request * passage_len, kv_local, head_dim)
    )
    value_part = (
        plain[..., 1, :]
        .astype(jnp.bfloat16)
        .reshape(requests, per_request * passage_len, kv_local, head_dim)
    )
    question_rows = question_kv.reshape(requests, question_len, kv_local, 2, head_dim)
    key_rows = jnp.concatenate([key_part, question_rows[:, :, :, 0, :]], axis=1)
    value_rows = jnp.concatenate([value_part, question_rows[:, :, :, 1, :]], axis=1)
    query_rows = queries.reshape(requests, question_len, kv_local, groups, head_dim)

    def one_block(items):
        return attend(items[0], items[1], items[2])

    result = lax.map(
        one_block, (query_rows[:, None], key_rows[:, None], value_rows[:, None])
    )
    return result.reshape(requests * question_len, kv_local * groups * head_dim)


def rope_table():
    half = HD // 2
    freqs = np.exp(
        np.arange(half, dtype=np.float32)
        * np.float32(-2.0 * np.log(np.float32(rope_theta)) / np.float32(HD))
    ).astype(np.float32)
    angles = (np.arange(NPAS, dtype=np.float32) * np.float32(PLEN))[:, None] * freqs[None, :]
    angles = angles.astype(np.float64)
    cosine = np.concatenate([np.cos(angles), np.cos(angles)], axis=1)
    sine = np.concatenate([-np.sin(angles), np.sin(angles)], axis=1)
    return np.stack([cosine, sine] * 4, axis=1).astype(np.float32)


def kernel(
    ids_ref, pages_ref, scales_ref, q_ref, qkv_ref, rope_ref,
    out_ref, flag_ref,
    p0, p1, p2, p3, yk1, yk2, yk3, yv1, yv2, yv3, gk0, gk1, gk2, gk3, gv0, gv1, gv2, gv3,
    s0, s1, s2, s3, s4, s5, s6, s7, l0, l1, l2, l3, l4, l5, l6, l7,
    idv, ids, want, mine, rope, queries, question, keys, values, probs, result,
    y_send, y_recv, x_send, x_recv, z_send, z_recv, i_send, i_recv, in_sem, out_sem,
):
    parts = (p0, p1, p2, p3)
    outward = (None, yk1, yk2, yk3, None, yv1, yv2, yv3)
    gathered = (gk0, gk1, gk2, gk3, gv0, gv1, gv2, gv3)
    outgoing = (s0, s1, s2, s3, s4, s5, s6, s7)
    landed = (l0, l1, l2, l3, l4, l5, l6, l7)
    store, head = lax.axis_index("store"), lax.axis_index("head")
    x, z, core = store // (ZS * CORES), (store // CORES) % ZS, store % CORES
    turn = 1 - 2 * core

    def at(x_, z_, core_):
        return ((x_ + 2 * XS) % XS * ZS + z_ % ZS) * CORES + core_

    def spot(x_, core_):
        return (x_ + 2 * XS) % XS * CORES + core_

    here = spot(x, core)

    barrier = pltpu.get_barrier_semaphore()
    peers = [(store, (head + c) % HEADS) for c in range(1, HEADS)]
    peers += [(at(x + 1, z, core), head), (at(x - 1, z, core), head), (at(x, z, 1 - core), head)]
    peers += [(at(x, z + d, core), head) for d in range(1, ZS)]
    for peer in peers:
        pl.semaphore_signal(barrier, inc=1, device_id=peer, device_id_type=MESH)

    def page_copy(c):
        to = (head + HEADS - c) % HEADS
        lanes = pl.ds(pl.multiple_of(to * PART, PART), PART)
        return pltpu.make_async_copy(pages_ref.at[:, lanes], parts[c], in_sem.at[c])

    for c in range(HEADS):
        page_copy(c).start()
    rope_copy = pltpu.make_async_copy(rope_ref, rope, in_sem.at[HEADS])
    query_copy = pltpu.make_async_copy(q_ref, queries, in_sem.at[HEADS + 1])
    question_copy = pltpu.make_async_copy(qkv_ref, question, in_sem.at[HEADS + 2])
    rope_copy.start()
    query_copy.start()
    question_copy.start()

    planes, over = [], 0
    for i in range(FETCH):
        one = ids_ref[i // NPAS, i % NPAS]
        plane = (one // P_DEV // CORES) % ZS
        rank = 0
        for other in planes:
            rank = rank + jnp.where(other == plane, 1, 0)
        planes.append(plane)
        over = jnp.maximum(over, rank)
        mine[i] = plane * SLOTS + jnp.minimum(rank, SLOTS - 1)
    lane8 = lax.broadcasted_iota(jnp.int32, (8, 128), 1)
    tile = jnp.where(lane8 == FETCH, over, 0)
    for i in range(FETCH):
        tile = jnp.where(lane8 == i, ids_ref[i // NPAS, i % NPAS], tile)
    idv[z] = tile

    def id_copy(step):
        return pltpu.make_async_remote_copy(
            src_ref=idv.at[z], dst_ref=idv.at[z],
            send_sem=i_send.at[step], recv_sem=i_recv.at[step],
            device_id=(at(x, z + step, core), head), device_id_type=MESH,
        )

    def y_copy(n):
        c = n % HEADS
        to = (head + HEADS - c) % HEADS
        return pltpu.make_async_remote_copy(
            src_ref=outward[n], dst_ref=gathered[n].at[here],
            send_sem=y_send.at[n], recv_sem=y_recv.at[n],
            device_id=(store, to), device_id_type=MESH,
        )

    def x_copy(n, kind):
        slot, to = (
            (here, at(x + 1, z, core)),
            (here, at(x - 1, z, core)),
            (spot(x - turn, core), at(x + turn, z, core)),
            (here, at(x, z, 1 - core)),
            (spot(x - 1, core), at(x, z, 1 - core)),
            (spot(x + 1, core), at(x, z, 1 - core)),
            (spot(x + 2, core), at(x, z, 1 - core)),
        )[kind]
        return pltpu.make_async_remote_copy(
            src_ref=gathered[n].at[slot], dst_ref=gathered[n].at[slot],
            send_sem=x_send.at[n, kind], recv_sem=x_recv.at[n, kind],
            device_id=(to, head), device_id_type=MESH,
        )

    def z_copy(n, step):
        return pltpu.make_async_remote_copy(
            src_ref=outgoing[n].at[step], dst_ref=landed[n].at[z],
            send_sem=z_send.at[n, step], recv_sem=z_recv.at[n, step],
            device_id=(at(x, z + step, core), head), device_id_type=MESH,
        )

    lane = lax.broadcasted_iota(jnp.int32, (TOK, 128), 1)
    pick_row = lax.broadcasted_iota(jnp.int32, (P_DEV * 2 * KVH, 128), 0)
    pick_lane = lax.broadcasted_iota(jnp.int32, (P_DEV * 2 * KVH, 128), 1)

    def scales_of(col):
        pick = jnp.where(pick_row == 2 * KVH * pick_lane + col, 1.0, 0.0).astype(jnp.bfloat16)
        return lax.dot_general(
            scales_ref[...], pick, (((0,), (0,)), ((), ())), preferred_element_type=jnp.float32
        )

    def lay_out(c, key_blocks, value_blocks, *at_):
        first = 4 * ((head + HEADS - c) % HEADS)
        scales = [scales_of(first + j) for j in range(4)]
        key_blocks[(*at_, P_DEV)] = jnp.concatenate([scales[0], scales[2]], axis=0).astype(jnp.bfloat16)

        def two_pages(i, carry):
            pair = pl.ds(pl.multiple_of(i * ROWS, ROWS), ROWS)
            codes = [
                parts[c][pair, LANES * g : LANES * (g + 1)].astype(jnp.float32) for g in range(2)
            ]
            for half in range(2):
                p, rows = 2 * i + half, slice(half * TOK, (half + 1) * TOK)
                value_half = []
                for g in range(2):
                    scale = jnp.sum(
                        jnp.where(lane == p, scales[2 * g + 1], 0.0), axis=1, keepdims=True
                    )
                    value_half.append(codes[g][rows, HD:] * scale)
                key_half = [codes[g][rows, :HD] for g in range(2)]
                key_blocks[(*at_, p)] = jnp.concatenate(key_half, axis=0).astype(jnp.bfloat16)
                value_blocks[(*at_, p)] = jnp.concatenate(value_half, axis=0).astype(jnp.bfloat16)
            return carry

        lax.fori_loop(0, P_DEV // 2, two_pages, 0)

    def x_start(n):
        if n % HEADS > 0:
            y_copy(n).wait_recv()
        if n == HEADS - 1:
            gk3[here, P_DEV, :, HD // 2 :] = jnp.broadcast_to(flag, (ROWS, HD // 2)).astype(
                jnp.bfloat16
            )
        for kind in (0, 1, 3):
            x_copy(n, kind).start()

    def x_forward(n):
        x_copy(n, 0).wait_recv()
        x_copy(n, 1).wait_recv()
        for kind in (2, 4, 5):
            x_copy(n, kind).start()

    def x_last(n):
        x_copy(n, 2).wait_recv()
        x_copy(n, 6).start()

    def x_done(n):
        for kind in (3, 4, 5, 6):
            x_copy(n, kind).wait_recv()

    rows_lane = lax.broadcasted_iota(jnp.int32, (ROWS, 128), 1)

    def finished(n, code):
        slot = code % P_DEV
        shard = (code // P_DEV) % (XS * ZS * CORES)
        k = code // (XS * ZS * CORES * P_DEV)
        place = (shard // (ZS * CORES)) * CORES + shard % CORES
        block = gathered[n][place, slot]
        if n >= HEADS:
            return block
        scales = gathered[n][place, P_DEV].astype(jnp.float32)
        scale = jnp.sum(jnp.where(rows_lane == slot, scales, 0.0), axis=1, keepdims=True)
        key = block.astype(jnp.float32) * scale
        turned = key * rope[k, 0:1] + pltpu.roll(key, HD // 2, 1) * rope[k, 1:2]
        return turned.astype(jnp.bfloat16)

    def z_start(n):
        def one_dest(i, carry):
            step = (i * 3) % ZS
            to = (z + step) % ZS
            for j in range(SLOTS):
                outgoing[n][step, j] = finished(n, want[to * SLOTS + j])
            z_copy(n, step).start()
            return carry

        lax.fori_loop(1, ZS, one_dest, 0)
        for j in range(SLOTS):
            landed[n][z, j] = finished(n, want[z * SLOTS + j])

    page_copy(0).wait()
    lay_out(0, gk0, gv0, here)
    pl.semaphore_wait(barrier, len(peers))
    for step in range(1, ZS):
        id_copy(step).start()
    x_start(0)
    for c in range(1, HEADS):
        page_copy(c).wait()
        lay_out(c, outward[c], outward[HEADS + c])
        y_copy(c).start()
    for c in range(1, HEADS):
        y_copy(HEADS + c).start()
    rope_copy.wait()

    for step in range(1, ZS):
        id_copy(step).wait_recv()
    to_smem = pltpu.make_async_copy(idv, ids, in_sem.at[HEADS + 3])
    to_smem.start()
    to_smem.wait()

    def scan(dest, worst):
        count = 0
        chosen = [0] * SLOTS
        for i in range(FETCH):
            one = ids[dest, 0, i]
            hit = (one // P_DEV // CORES) % ZS == z
            for j in range(SLOTS):
                chosen[j] = jnp.where(
                    hit & (count == j), one + (i % NPAS) * (XS * ZS * CORES * P_DEV), chosen[j]
                )
            count = count + jnp.where(hit, 1, 0)
        for j in range(SLOTS):
            want[dest * SLOTS + j] = chosen[j]
        return jnp.maximum(worst, ids[dest, 0, FETCH])

    x_forward(0)
    worst = lax.fori_loop(0, ZS, scan, jnp.int32(0))
    flag = jnp.where(worst >= SLOTS, 1.0, 0.0)

    for n in range(CHUNKS):
        if n > 0:
            x_forward(n)
        if n + 1 < CHUNKS:
            x_start(n + 1)
        x_last(n)
        x_done(n)
        z_start(n)

    flags = gk3[0, P_DEV].astype(jnp.float32)
    for place in range(1, SHARDS):
        flags = jnp.maximum(flags, gk3[place, P_DEV].astype(jnp.float32))
    flag_ref[...] = flags[:8]

    def arrived(n):
        def one(step, carry):
            z_copy(n, step).wait_recv()
            return carry

        lax.fori_loop(1, ZS, one, 0)

    def passages(n, r):
        blocks = []
        for k in range(NPAS):
            place = mine[r * NPAS + k]
            blocks.append(landed[n][place // SLOTS, place % SLOTS].astype(jnp.float32))
        return [
            jnp.concatenate([b[g * TOK : (g + 1) * TOK] for b in blocks], axis=0).astype(
                jnp.bfloat16
            )
            for g in range(2)
        ]

    for c in range(HEADS):
        arrived(c)
    query_copy.wait()
    question_copy.wait()

    col = lax.broadcasted_iota(jnp.int32, (GROUPS * QLEN, QLEN), 1)
    row = lax.broadcasted_iota(jnp.int32, (GROUPS * QLEN, QLEN), 0) % QLEN
    seen = col <= row

    def weigh(r, carry):
        rows = pl.ds(pl.multiple_of(r * QLEN, QLEN), QLEN)
        for c in range(HEADS):
            for g, part in enumerate(passages(c, r)):
                keys[g, c * PIECE : (c + 1) * PIECE, :] = part
        for g in range(2):
            keys[g, PKEYS:, :] = question[rows, g * LANES : g * LANES + HD]
            values[r, g, PKEYS:, :] = question[rows, g * LANES + HD : (g + 1) * LANES]
            query = jnp.concatenate(
                [
                    queries[rows, (g * GROUPS + j) * HD : (g * GROUPS + j + 1) * HD]
                    for j in range(GROUPS)
                ],
                axis=0,
            )
            dims = (((1,), (1,)), ((), ()))
            scale = jnp.float32(1.0 / math.sqrt(HD))
            past = scale * lax.dot_general(
                query, keys[g, :PKEYS, :], dims, preferred_element_type=jnp.float32
            )
            now = scale * lax.dot_general(
                query, keys[g, PKEYS:, :], dims, preferred_element_type=jnp.float32
            )
            now = jnp.where(seen, now, -jnp.inf)
            top = jnp.maximum(
                jnp.max(past, axis=1, keepdims=True), jnp.max(now, axis=1, keepdims=True)
            )
            past = jnp.exp(past - top)
            now = jnp.exp(now - top)
            total = jnp.sum(past, axis=1, keepdims=True) + jnp.sum(now, axis=1, keepdims=True)
            inverse = 1.0 / total
            probs[r, g, :, :PKEYS] = (past * inverse).astype(jnp.bfloat16)
            probs[r, g, :, PKEYS:] = (now * inverse).astype(jnp.bfloat16)
        return carry

    lax.fori_loop(0, R_DEV, weigh, 0)

    for c in range(HEADS):
        arrived(HEADS + c)

        def place_values(r, carry, c=c):
            for g, part in enumerate(passages(HEADS + c, r)):
                values[r, g, c * PIECE : (c + 1) * PIECE, :] = part
            return carry

        lax.fori_loop(0, R_DEV, place_values, 0)

    def out_copy(r):
        rows = pl.ds(pl.multiple_of(r * QLEN, QLEN), QLEN)
        return pltpu.make_async_copy(result.at[r], out_ref.at[rows], out_sem.at[r])

    def mix(r, carry):
        for g in range(2):
            mixed = jnp.dot(probs[r, g], values[r, g], preferred_element_type=jnp.float32)
            for j in range(GROUPS):
                result[r, :, (g * GROUPS + j) * HD : (g * GROUPS + j + 1) * HD] = mixed[
                    j * QLEN : (j + 1) * QLEN
                ].astype(jnp.bfloat16)
        out_copy(r).start()
        return carry

    lax.fori_loop(0, R_DEV, mix, 0)

    for step in range(1, ZS):
        id_copy(step).wait_send()
    for n in range(CHUNKS):
        if n % HEADS > 0:
            y_copy(n).wait_send()
        for kind in range(7):
            x_copy(n, kind).wait_send()
        for step in range(1, ZS):
            z_copy(n, step).wait_send()
    for r in range(R_DEV):
        out_copy(r).wait()


def fast(queries, question_kv, pages, page_scales, passage_ids):
    vmem = pl.BlockSpec(memory_space=pltpu.VMEM)
    hbm = pl.BlockSpec(memory_space=pl.ANY)
    block = (ROWS, HD)
    dma, bf16 = pltpu.SemaphoreType.DMA, jnp.bfloat16
    rows = pages.reshape(P_DEV * TOK, 2 * KVH * HD)
    scales = page_scales.transpose(0, 2, 1).reshape(P_DEV * 2 * KVH, TOK)
    return pl.pallas_call(
        kernel,
        out_shape=(
            jax.ShapeDtypeStruct(queries.shape, bf16),
            jax.ShapeDtypeStruct((8, 128), jnp.float32),
        ),
        in_specs=[pl.BlockSpec(memory_space=pltpu.SMEM), hbm, vmem, hbm, hbm, hbm],
        out_specs=(hbm, vmem),
        scratch_shapes=[pltpu.VMEM((P_DEV * TOK, PART), bf16)] * HEADS
        + [pltpu.VMEM((P_DEV + 1,) + block, bf16)] * (HEADS - 1)
        + [pltpu.VMEM((P_DEV,) + block, bf16)] * (HEADS - 1)
        + [pltpu.VMEM((SHARDS, P_DEV + 1) + block, bf16)] * HEADS
        + [pltpu.VMEM((SHARDS, P_DEV) + block, bf16)] * HEADS
        + [pltpu.VMEM((ZS, SLOTS) + block, bf16)] * (2 * CHUNKS)
        + [
            pltpu.VMEM((ZS, 8, 128), jnp.int32),
            pltpu.SMEM((ZS, 8, 128), jnp.int32),
            pltpu.SMEM((ZS * SLOTS,), jnp.int32),
            pltpu.SMEM((FETCH,), jnp.int32),
            pltpu.VMEM((NPAS, 8, HD), jnp.float32),
            pltpu.VMEM(queries.shape, bf16),
            pltpu.VMEM(question_kv.shape, bf16),
            pltpu.VMEM((2, KEYS, HD), bf16),
            pltpu.VMEM((R_DEV, 2, KEYS, HD), bf16),
            pltpu.VMEM((R_DEV, 2, GROUPS * QLEN, KEYS), bf16),
            pltpu.VMEM((R_DEV, QLEN, QH // HEADS * HD), bf16),
            dma((CHUNKS,)), dma((CHUNKS,)),
            dma((CHUNKS, 7)), dma((CHUNKS, 7)),
            dma((CHUNKS, ZS)), dma((CHUNKS, ZS)),
            dma((ZS,)), dma((ZS,)),
            dma((HEADS + 4,)), dma((R_DEV,)),
        ],
        compiler_params=pltpu.CompilerParams(
            collective_id=0, has_side_effects=True, vmem_limit_bytes=48 * 1024 * 1024
        ),
    )(passage_ids, rows, scales, queries, question_kv, jnp.asarray(rope_table()))


def per_device(queries, question_kv, pages, page_scales, passage_ids):
    args = (queries, question_kv, pages, page_scales, passage_ids)
    result, flags = fast(*args)
    return lax.cond(flags[0, HD - 1] > 0, lambda: general(*args), lambda: result)


def solution(mesh):
    return jax.shard_map(
        per_device,
        mesh=mesh,
        in_specs=(
            P("store", "head"),
            P("store", "head"),
            P("store", "head", None),
            P("store", "head", None),
            P("store", None),
        ),
        out_specs=P("store", "head"),
        check_vma=False,
    )
```

```python
import math

import numpy as np
import jax
import jax.numpy as jnp
from jax import lax
from jax.experimental import pallas as pl
from jax.experimental.pallas import tpu as pltpu
from jax.sharding import PartitionSpec as P

QH = 64
KVH = 8
HD = 128
NPAS = 4
PLEN = 96
CAP = 2
QLEN = 64
R_DEV = 4
P_DEV = 16
XS, ZS, CORES, HEADS = 4, 8, 2, 4
SHARDS = XS * CORES
TOK = PLEN // HEADS
ROWS = 2 * TOK
LANES = 2 * HD
SLOTS = 4
FETCH = R_DEV * NPAS
GROUPS = QH // KVH
PART = 4 * HD
PIECE = NPAS * TOK
PKEYS = NPAS * PLEN
KEYS = PKEYS + QLEN
CHUNKS = 2 * HEADS + 1
REST = CHUNKS - 1
FIRST = 16
ORDER = (0, REST, 4, 1, 3, 2, 5, 7, 6)
LAST = ORDER[-1] - HEADS
MESH = pl.DeviceIdType.MESH

rope_theta = 500000.0


def rows_of(n):
    return FIRST if n == 0 else ROWS - FIRST if n == REST else ROWS


def holds_keys(n):
    return n < HEADS or n == REST


def rotate_keys(keys, offsets):
    half_dim = keys.shape[-1] // 2
    freqs = jnp.exp(
        jnp.arange(half_dim, dtype=jnp.float32)
        * (-2.0 * jnp.log(jnp.float32(rope_theta)) / keys.shape[-1])
    )
    angles = offsets[:, None] * freqs[None, :]
    cosine = jnp.cos(angles)[:, None, None, :]
    sine = jnp.sin(angles)[:, None, None, :]
    first = keys[..., :half_dim]
    second = keys[..., half_dim:]
    return jnp.concatenate(
        [first * cosine - second * sine, second * cosine + first * sine], axis=-1
    )


def attend(query_rows, key_rows, value_rows):
    qlen = query_rows.shape[1]
    total = key_rows.shape[1]
    scores = jnp.einsum(
        "bqkgd,bskd->bkgqs", query_rows, key_rows, preferred_element_type=jnp.float32
    ) / jnp.sqrt(jnp.float32(query_rows.shape[-1]))
    key_pos = jnp.arange(total)
    query_pos = jnp.arange(qlen) + (total - qlen)
    allowed = key_pos[None, :] <= query_pos[:, None]
    scores = jnp.where(allowed, scores, -jnp.inf)
    highest = jnp.max(scores, axis=-1, keepdims=True)
    raised = jnp.exp(scores - highest)
    probs = (raised / jnp.sum(raised, axis=-1, keepdims=True)).astype(jnp.bfloat16)
    result = jnp.einsum("bkgqs,bskd->bqkgd", probs, value_rows, preferred_element_type=jnp.float32)
    return result.astype(jnp.bfloat16)


def general(queries, question_kv, pages, page_scales, passage_ids):
    shards = lax.axis_size("store")
    groups_axis = lax.axis_size("head")
    requests, per_request = passage_ids.shape
    fetches = requests * per_request
    stored, part_tokens, lanes = pages.shape
    passage_len = part_tokens * groups_axis
    kv_local = KVH // groups_axis
    groups = QH // KVH
    head_dim = HD
    question_len = queries.shape[0] // requests
    flat_ids = passage_ids.reshape(fetches)
    shard_of = flat_ids // stored
    within = flat_ids % stored
    counter = jnp.arange(fetches)
    same_shard = shard_of[:, None] == shard_of[None, :]
    earlier = counter[None, :] < counter[:, None]
    order_rank = jnp.sum(same_shard & earlier, axis=1)
    slot_index = shard_of * CAP + order_rank
    matches = slot_index[:, None] == jnp.arange(shards * CAP)[None, :]
    wanted_table = jnp.sum(jnp.where(matches, within[:, None], 0), axis=0).reshape(shards, CAP)
    asked = lax.all_to_all(wanted_table, "store", split_axis=0, concat_axis=0, tiled=True)
    asked_flat = asked.reshape(shards * CAP)
    send_pages = jnp.take(pages, asked_flat, axis=0).reshape(shards, CAP, part_tokens, lanes)
    send_scales = jnp.take(page_scales, asked_flat, axis=0).reshape(
        shards, CAP, part_tokens, 2 * KVH
    )
    got_pages, got_scales = (
        lax.all_to_all(
            lax.all_to_all(send_pages, "store", split_axis=0, concat_axis=0, tiled=True),
            "head",
            split_axis=3,
            concat_axis=2,
            tiled=True,
        ),
        lax.all_to_all(
            lax.all_to_all(send_scales, "store", split_axis=0, concat_axis=0, tiled=True),
            "head",
            split_axis=3,
            concat_axis=2,
            tiled=True,
        ),
    )
    mine_pages = jnp.take(
        got_pages.reshape(shards * CAP, passage_len, 2 * kv_local * head_dim), slot_index, axis=0
    )
    mine_scales = jnp.take(
        got_scales.reshape(shards * CAP, passage_len, 2 * kv_local), slot_index, axis=0
    )
    mine_pages = mine_pages.reshape(requests, per_request, passage_len, kv_local, 2, head_dim)
    mine_scales = mine_scales.reshape(requests, per_request, passage_len, kv_local, 2)
    plain = mine_pages.astype(jnp.float32) * mine_scales.astype(jnp.float32)[..., None]
    offsets = jnp.arange(per_request, dtype=jnp.float32) * passage_len
    key_part = (
        rotate_keys(plain[..., 0, :], offsets)
        .astype(jnp.bfloat16)
        .reshape(requests, per_request * passage_len, kv_local, head_dim)
    )
    value_part = (
        plain[..., 1, :]
        .astype(jnp.bfloat16)
        .reshape(requests, per_request * passage_len, kv_local, head_dim)
    )
    question_rows = question_kv.reshape(requests, question_len, kv_local, 2, head_dim)
    key_rows = jnp.concatenate([key_part, question_rows[:, :, :, 0, :]], axis=1)
    value_rows = jnp.concatenate([value_part, question_rows[:, :, :, 1, :]], axis=1)
    query_rows = queries.reshape(requests, question_len, kv_local, groups, head_dim)

    def one_block(items):
        return attend(items[0], items[1], items[2])

    result = lax.map(
        one_block, (query_rows[:, None], key_rows[:, None], value_rows[:, None])
    )
    return result.reshape(requests * question_len, kv_local * groups * head_dim)


def rope_table():
    half = HD // 2
    freqs = np.exp(
        np.arange(half, dtype=np.float32)
        * np.float32(-2.0 * np.log(np.float32(rope_theta)) / np.float32(HD))
    ).astype(np.float32)
    angles = (np.arange(NPAS, dtype=np.float32) * np.float32(PLEN))[:, None] * freqs[None, :]
    angles = angles.astype(np.float64)
    cosine = np.concatenate([np.cos(angles), np.cos(angles)], axis=1)
    sine = np.concatenate([-np.sin(angles), np.sin(angles)], axis=1)
    return np.stack([cosine, sine] * 4, axis=1).astype(np.float32)


def kernel(
    ids_ref, pages_ref, scales_ref, q_ref, qkv_ref, rope_ref,
    out_ref, flag_ref,
    p0, p1, p2, p3, yk1, yk2, yk3, yv1, yv2, yv3, gk0, gk1, gk2, gk3, gv0, gv1, gv2, gv3, gk4,
    s0, s1, s2, s3, s4, s5, s6, s7, s8, l0, l1, l2, l3, l4, l5, l6, l7, l8,
    idv, ids, mine, rope, scaling, queries, question, keys, values, late, probs, late_probs, sums,
    result,
    y_send, y_recv, x_send, x_recv, z_send, z_recv, i_send, i_recv, in_sem, out_sem,
):
    parts = (p0, p1, p2, p3)
    outward = (None, yk1, yk2, yk3, None, yv1, yv2, yv3, None)
    gathered = (gk0, gk1, gk2, gk3, gv0, gv1, gv2, gv3, gk4)
    outgoing = (s0, s1, s2, s3, s4, s5, s6, s7, s8)
    landed = (l0, l1, l2, l3, l4, l5, l6, l7, l8)
    store, head = lax.axis_index("store"), lax.axis_index("head")
    x, z, core = store // (ZS * CORES), (store // CORES) % ZS, store % CORES
    turn = 1 - 2 * core

    def at(x_, z_, core_):
        return ((x_ + 2 * XS) % XS * ZS + z_ % ZS) * CORES + core_

    def spot(x_, core_):
        return (x_ + 2 * XS) % XS * CORES + core_

    here = spot(x, core)

    barrier = pltpu.get_barrier_semaphore()
    peers = [(store, (head + c) % HEADS) for c in range(1, HEADS)]
    peers += [(at(x + 1, z, core), head), (at(x - 1, z, core), head), (at(x, z, 1 - core), head)]
    peers += [(at(x, z + d, core), head) for d in range(1, ZS)]
    for peer in peers:
        pl.semaphore_signal(barrier, inc=1, device_id=peer, device_id_type=MESH)

    def page_copy(c):
        to = (head + HEADS - c) % HEADS
        lanes = pl.ds(pl.multiple_of(to * PART, PART), PART)
        return pltpu.make_async_copy(pages_ref.at[:, lanes], parts[c], in_sem.at[c])

    scale_copy = pltpu.make_async_copy(scales_ref, scaling, in_sem.at[HEADS + 4])
    scale_copy.start()
    for c in range(HEADS):
        page_copy(c).start()
    rope_copy = pltpu.make_async_copy(rope_ref, rope, in_sem.at[HEADS])
    query_copy = pltpu.make_async_copy(q_ref, queries, in_sem.at[HEADS + 1])
    question_copy = pltpu.make_async_copy(qkv_ref, question, in_sem.at[HEADS + 2])
    rope_copy.start()
    query_copy.start()
    question_copy.start()

    planes, over = [], 0
    lane8 = lax.broadcasted_iota(jnp.int32, (8, 128), 1)
    row8 = lax.broadcasted_iota(jnp.int32, (8, 128), 0)
    tile = jnp.zeros((8, 128), jnp.int32)
    for i in range(FETCH):
        one = ids_ref[i // NPAS, i % NPAS]
        plane = (one // P_DEV // CORES) % ZS
        rank = 0
        for other in planes:
            rank = rank + jnp.where(other == plane, 1, 0)
        planes.append(plane)
        over = jnp.maximum(over, rank)
        mine[i] = plane * SLOTS + jnp.minimum(rank, SLOTS - 1)
        code = one + (i % NPAS) * (XS * ZS * CORES * P_DEV)
        tile = jnp.where((lane8 == rank) & (row8 == plane), code, tile)
    idv[z] = jnp.where(lane8 == FETCH, over, tile)

    def id_copy(step):
        return pltpu.make_async_remote_copy(
            src_ref=idv.at[z], dst_ref=idv.at[z],
            send_sem=i_send.at[step], recv_sem=i_recv.at[step],
            device_id=(at(x, z + step, core), head), device_id_type=MESH,
        )

    def y_copy(n):
        c = n % HEADS
        to = (head + HEADS - c) % HEADS
        return pltpu.make_async_remote_copy(
            src_ref=outward[n], dst_ref=gathered[n].at[here],
            send_sem=y_send.at[n], recv_sem=y_recv.at[n],
            device_id=(store, to), device_id_type=MESH,
        )

    def x_copy(n, kind):
        slot, to = (
            (here, at(x + 1, z, core)),
            (here, at(x - 1, z, core)),
            (spot(x - turn, core), at(x + turn, z, core)),
            (here, at(x, z, 1 - core)),
            (spot(x - 1, core), at(x, z, 1 - core)),
            (spot(x + 1, core), at(x, z, 1 - core)),
            (spot(x + 2, core), at(x, z, 1 - core)),
        )[kind]
        return pltpu.make_async_remote_copy(
            src_ref=gathered[n].at[slot], dst_ref=gathered[n].at[slot],
            send_sem=x_send.at[n, kind], recv_sem=x_recv.at[n, kind],
            device_id=(to, head), device_id_type=MESH,
        )

    def z_copy(n, step):
        return pltpu.make_async_remote_copy(
            src_ref=outgoing[n].at[step], dst_ref=landed[n].at[z],
            send_sem=z_send.at[n, step], recv_sem=z_recv.at[n, step],
            device_id=(at(x, z + step, core), head), device_id_type=MESH,
        )

    lane = lax.broadcasted_iota(jnp.int32, (TOK, 128), 1)
    pick_row = lax.broadcasted_iota(jnp.int32, (P_DEV * 2 * KVH, 128), 0)
    pick_lane = lax.broadcasted_iota(jnp.int32, (P_DEV * 2 * KVH, 128), 1)

    def scales_of(col):
        pick = jnp.where(pick_row == 2 * KVH * pick_lane + col, 1.0, 0.0).astype(jnp.bfloat16)
        return lax.dot_general(
            scaling[...], pick, (((0,), (0,)), ((), ())), preferred_element_type=jnp.float32
        )

    def lay_out(c):
        first = 4 * ((head + HEADS - c) % HEADS)
        scales = [scales_of(first + j) for j in range(4)]

        def put_keys(p, rows):
            if c == 0:
                gk0[here, p] = rows[:FIRST].astype(jnp.bfloat16)
                gk4[here, p] = rows[FIRST:].astype(jnp.bfloat16)
            else:
                outward[c][p] = rows.astype(jnp.bfloat16)

        def put_values(p, rows):
            if c == 0:
                gv0[here, p] = rows.astype(jnp.bfloat16)
            else:
                outward[HEADS + c][p] = rows.astype(jnp.bfloat16)

        put_keys(P_DEV, jnp.concatenate([scales[0], scales[2]], axis=0))

        def two_pages(i, carry):
            pair = pl.ds(pl.multiple_of(i * ROWS, ROWS), ROWS)
            codes = [
                parts[c][pair, LANES * g : LANES * (g + 1)].astype(jnp.float32) for g in range(2)
            ]
            for half in range(2):
                p, rows = 2 * i + half, slice(half * TOK, (half + 1) * TOK)
                value_half = []
                for g in range(2):
                    scale = jnp.sum(
                        jnp.where(lane == p, scales[2 * g + 1], 0.0), axis=1, keepdims=True
                    )
                    value_half.append(codes[g][rows, HD:] * scale)
                put_keys(p, jnp.concatenate([codes[g][rows, :HD] for g in range(2)], axis=0))
                put_values(p, jnp.concatenate(value_half, axis=0))
            return carry

        lax.fori_loop(0, P_DEV // 2, two_pages, 0)

    def x_start(n):
        if n % HEADS > 0:
            y_copy(n).wait_recv()
        if n == HEADS - 1:
            gk3[here, P_DEV, :, HD // 2 :] = jnp.broadcast_to(flag, (ROWS, HD // 2)).astype(
                jnp.bfloat16
            )
        for kind in (0, 1, 3):
            x_copy(n, kind).start()

    def x_forward(n):
        x_copy(n, 0).wait_recv()
        x_copy(n, 1).wait_recv()
        for kind in (2, 4, 5):
            x_copy(n, kind).start()

    def x_last(n):
        x_copy(n, 2).wait_recv()
        x_copy(n, 6).start()

    def x_done(n):
        for kind in (3, 4, 5, 6):
            x_copy(n, kind).wait_recv()

    def finished(n, code):
        slot = code % P_DEV
        shard = (code // P_DEV) % (XS * ZS * CORES)
        k = code // (XS * ZS * CORES * P_DEV)
        place = (shard // (ZS * CORES)) * CORES + shard % CORES
        block = gathered[n][place, slot]
        if not holds_keys(n):
            return block
        rows_lane = lax.broadcasted_iota(jnp.int32, (rows_of(n), 128), 1)
        scales = gathered[n][place, P_DEV].astype(jnp.float32)
        scale = jnp.sum(jnp.where(rows_lane == slot, scales, 0.0), axis=1, keepdims=True)
        key = block.astype(jnp.float32) * scale
        turned = key * rope[k, 0:1] + pltpu.roll(key, HD // 2, 1) * rope[k, 1:2]
        return turned.astype(jnp.bfloat16)

    def z_start(n):
        def one_dest(i, carry):
            step = (i * 3) % ZS
            to = (z + step) % ZS
            for j in range(SLOTS):
                outgoing[n][step, j] = finished(n, ids[to, z, j])
            z_copy(n, step).start()
            return carry

        lax.fori_loop(1, ZS, one_dest, 0)
        for j in range(SLOTS):
            landed[n][z, j] = finished(n, ids[z, z, j])

    scale_copy.wait()
    page_copy(0).wait()
    lay_out(0)
    pl.semaphore_wait(barrier, len(peers))
    for step in range(1, ZS):
        id_copy(step).start()
    x_start(ORDER[0])
    x_start(ORDER[1])
    for c in (1, 3, 2):
        page_copy(c).wait()
        lay_out(c)
        y_copy(c).start()
    rope_copy.wait()

    for step in range(1, ZS):
        id_copy(step).wait_recv()
    to_smem = pltpu.make_async_copy(idv, ids, in_sem.at[HEADS + 3])
    to_smem.start()
    to_smem.wait()

    x_forward(0)
    worst = ids[0, 0, FETCH]
    for dest in range(1, ZS):
        worst = jnp.maximum(worst, ids[dest, 0, FETCH])
    flag = jnp.where(worst >= SLOTS, 1.0, 0.0)

    x_start(ORDER[2])
    x_last(0)
    x_forward(ORDER[1])
    x_done(0)
    z_start(0)
    x_start(ORDER[3])
    for n in ORDER[6:]:
        y_copy(n).start()
    for i in range(1, CHUNKS):
        x_last(ORDER[i])
        if i + 1 < CHUNKS:
            x_forward(ORDER[i + 1])
        if i + 3 < CHUNKS:
            x_start(ORDER[i + 3])
        x_done(ORDER[i])
        z_start(ORDER[i])

    flags = gk3[0, P_DEV].astype(jnp.float32)
    for place in range(1, SHARDS):
        flags = jnp.maximum(flags, gk3[place, P_DEV].astype(jnp.float32))
    flag_ref[...] = flags[:8]

    def arrived(n):
        def one(step, carry):
            z_copy(n, step).wait_recv()
            return carry

        lax.fori_loop(1, ZS, one, 0)

    def passages(ns, r):
        blocks = []
        for k in range(NPAS):
            place = mine[r * NPAS + k]
            pieces = [landed[n][place // SLOTS, place % SLOTS].astype(jnp.float32) for n in ns]
            blocks.append(pieces[0] if len(ns) == 1 else jnp.concatenate(pieces, axis=0))
        return [
            jnp.concatenate([b[g * TOK : (g + 1) * TOK] for b in blocks], axis=0).astype(
                jnp.bfloat16
            )
            for g in range(2)
        ]

    early = [c for c in (0, 1, 3, 2) if c != LAST]
    for n in [n for n in ORDER if holds_keys(n)]:
        arrived(n)
    query_copy.wait()
    question_copy.wait()

    col = lax.broadcasted_iota(jnp.int32, (GROUPS * QLEN, QLEN), 1)
    row = lax.broadcasted_iota(jnp.int32, (GROUPS * QLEN, QLEN), 0) % QLEN
    seen = col <= row

    def weigh(r, carry):
        rows = pl.ds(pl.multiple_of(r * QLEN, QLEN), QLEN)
        for i, c in enumerate(early + [LAST]):
            for g, part in enumerate(passages((0, REST) if c == 0 else (c,), r)):
                keys[g, i * PIECE : (i + 1) * PIECE, :] = part
        for g in range(2):
            keys[g, PKEYS:, :] = question[rows, g * LANES : g * LANES + HD]
            values[r, g, PKEYS - PIECE :, :] = question[rows, g * LANES + HD : (g + 1) * LANES]
            query = jnp.concatenate(
                [
                    queries[rows, (g * GROUPS + j) * HD : (g * GROUPS + j + 1) * HD]
                    for j in range(GROUPS)
                ],
                axis=0,
            )
            dims = (((1,), (1,)), ((), ()))
            scale = jnp.float32(1.0 / math.sqrt(HD))
            past = scale * lax.dot_general(
                query, keys[g, :PKEYS, :], dims, preferred_element_type=jnp.float32
            )
            now = scale * lax.dot_general(
                query, keys[g, PKEYS:, :], dims, preferred_element_type=jnp.float32
            )
            now = jnp.where(seen, now, -jnp.inf)
            top = jnp.maximum(
                jnp.max(past, axis=1, keepdims=True), jnp.max(now, axis=1, keepdims=True)
            )
            past = jnp.exp(past - top)
            now = jnp.exp(now - top)
            total = jnp.sum(past, axis=1, keepdims=True) + jnp.sum(now, axis=1, keepdims=True)
            inverse = 1.0 / total
            past = (past * inverse).astype(jnp.bfloat16)
            probs[r, g, :, : PKEYS - PIECE] = past[:, : PKEYS - PIECE]
            probs[r, g, :, PKEYS - PIECE :] = (now * inverse).astype(jnp.bfloat16)
            late_probs[r, g] = past[:, PKEYS - PIECE :]
        return carry

    lax.fori_loop(0, R_DEV, weigh, 0)

    for i, c in enumerate(early):
        arrived(HEADS + c)

        def place_values(r, carry, i=i, c=c):
            for g, part in enumerate(passages((HEADS + c,), r)):
                values[r, g, i * PIECE : (i + 1) * PIECE, :] = part
            return carry

        lax.fori_loop(0, R_DEV, place_values, 0)

    def mix_early(r, carry):
        for g in range(2):
            sums[r, g] = jnp.dot(probs[r, g], values[r, g], preferred_element_type=jnp.float32)
        return carry

    lax.fori_loop(0, R_DEV, mix_early, 0)
    arrived(HEADS + LAST)

    def out_copy(r):
        rows = pl.ds(pl.multiple_of(r * QLEN, QLEN), QLEN)
        return pltpu.make_async_copy(result.at[r], out_ref.at[rows], out_sem.at[r])

    def mix(r, carry):
        for g, part in enumerate(passages((HEADS + LAST,), r)):
            late[g] = part
        for g in range(2):
            mixed = sums[r, g] + jnp.dot(
                late_probs[r, g], late[g], preferred_element_type=jnp.float32
            )
            for j in range(GROUPS):
                result[r, :, (g * GROUPS + j) * HD : (g * GROUPS + j + 1) * HD] = mixed[
                    j * QLEN : (j + 1) * QLEN
                ].astype(jnp.bfloat16)
        out_copy(r).start()
        return carry

    lax.fori_loop(0, R_DEV, mix, 0)

    for step in range(1, ZS):
        id_copy(step).wait_send()
    for n in range(CHUNKS):
        if n % HEADS > 0:
            y_copy(n).wait_send()
        for kind in range(7):
            x_copy(n, kind).wait_send()
        for step in range(1, ZS):
            z_copy(n, step).wait_send()
    for r in range(R_DEV):
        out_copy(r).wait()


def fast(queries, question_kv, pages, page_scales, passage_ids):
    vmem = pl.BlockSpec(memory_space=pltpu.VMEM)
    hbm = pl.BlockSpec(memory_space=pl.ANY)
    block = (ROWS, HD)
    dma, bf16 = pltpu.SemaphoreType.DMA, jnp.bfloat16
    rows = pages.reshape(P_DEV * TOK, 2 * KVH * HD)
    scales = page_scales.transpose(0, 2, 1).reshape(P_DEV * 2 * KVH, TOK)
    return pl.pallas_call(
        kernel,
        out_shape=(
            jax.ShapeDtypeStruct(queries.shape, bf16),
            jax.ShapeDtypeStruct((8, 128), jnp.float32),
        ),
        in_specs=[pl.BlockSpec(memory_space=pltpu.SMEM)] + [hbm] * 5,
        out_specs=(hbm, vmem),
        scratch_shapes=[pltpu.VMEM((P_DEV * TOK, PART), bf16)] * HEADS
        + [pltpu.VMEM((P_DEV + 1,) + block, bf16)] * (HEADS - 1)
        + [pltpu.VMEM((P_DEV,) + block, bf16)] * (HEADS - 1)
        + [
            pltpu.VMEM((SHARDS, P_DEV + holds_keys(n), rows_of(n), HD), bf16)
            for n in range(CHUNKS)
        ]
        + [pltpu.VMEM((ZS, SLOTS, rows_of(n), HD), bf16) for n in range(CHUNKS)] * 2
        + [
            pltpu.VMEM((ZS, 8, 128), jnp.int32),
            pltpu.SMEM((ZS, 8, 128), jnp.int32),
            pltpu.SMEM((FETCH,), jnp.int32),
            pltpu.VMEM((NPAS, 8, HD), jnp.float32),
            pltpu.VMEM(scales.shape, bf16),
            pltpu.VMEM(queries.shape, bf16),
            pltpu.VMEM(question_kv.shape, bf16),
            pltpu.VMEM((2, KEYS, HD), bf16),
            pltpu.VMEM((R_DEV, 2, KEYS - PIECE, HD), bf16),
            pltpu.VMEM((2, PIECE, HD), bf16),
            pltpu.VMEM((R_DEV, 2, GROUPS * QLEN, KEYS - PIECE), bf16),
            pltpu.VMEM((R_DEV, 2, GROUPS * QLEN, PIECE), bf16),
            pltpu.VMEM((R_DEV, 2, GROUPS * QLEN, HD), jnp.float32),
            pltpu.VMEM((R_DEV, QLEN, QH // HEADS * HD), bf16),
            dma((CHUNKS,)), dma((CHUNKS,)),
            dma((CHUNKS, 7)), dma((CHUNKS, 7)),
            dma((CHUNKS, ZS)), dma((CHUNKS, ZS)),
            dma((ZS,)), dma((ZS,)),
            dma((HEADS + 5,)), dma((R_DEV,)),
        ],
        compiler_params=pltpu.CompilerParams(
            collective_id=0, has_side_effects=True, vmem_limit_bytes=58 * 1024 * 1024
        ),
    )(passage_ids, rows, scales, queries, question_kv, jnp.asarray(rope_table()))


def per_device(queries, question_kv, pages, page_scales, passage_ids):
    args = (queries, question_kv, pages, page_scales, passage_ids)
    result, flags = fast(*args)
    full = flags[0, HD - 1] > 0
    return lax.cond(full, lambda: general(*args), lambda: result)


def solution(mesh):
    return jax.shard_map(
        per_device,
        mesh=mesh,
        in_specs=(
            P("store", "head"),
            P("store", "head"),
            P("store", "head", None),
            P("store", "head", None),
            P("store", None),
        ),
        out_specs=P("store", "head"),
        check_vma=False,
    )
```

```python
import math

import numpy as np
import jax
import jax.numpy as jnp
from jax import lax
from jax.experimental import pallas as pl
from jax.experimental.pallas import tpu as pltpu
from jax.sharding import PartitionSpec as P

QH = 64
KVH = 8
HD = 128
NPAS = 4
PLEN = 96
CAP = 2
QLEN = 64
R_DEV = 4
P_DEV = 16
XS, ZS, CORES, HEADS = 4, 8, 2, 4
SHARDS = XS * CORES
TOK = PLEN // HEADS
ROWS = 2 * TOK
LANES = 2 * HD
SLOTS = 4
FETCH = R_DEV * NPAS
GROUPS = QH // KVH
PART = 4 * HD
PIECE = NPAS * TOK
PKEYS = NPAS * PLEN
KEYS = PKEYS + QLEN
CHUNKS = 2 * HEADS + 1
REST = CHUNKS - 1
FIRST = 16
ORDER = (0, REST, 4, 1, 3, 2, 5, 7, 6)
LAST = ORDER[-1] - HEADS
MESH = pl.DeviceIdType.MESH

rope_theta = 500000.0


def rows_of(n):
    return FIRST if n == 0 else ROWS - FIRST if n == REST else ROWS


def holds_keys(n):
    return n < HEADS or n == REST


def rotate_keys(keys, offsets):
    half_dim = keys.shape[-1] // 2
    freqs = jnp.exp(
        jnp.arange(half_dim, dtype=jnp.float32)
        * (-2.0 * jnp.log(jnp.float32(rope_theta)) / keys.shape[-1])
    )
    angles = offsets[:, None] * freqs[None, :]
    cosine = jnp.cos(angles)[:, None, None, :]
    sine = jnp.sin(angles)[:, None, None, :]
    first = keys[..., :half_dim]
    second = keys[..., half_dim:]
    return jnp.concatenate(
        [first * cosine - second * sine, second * cosine + first * sine], axis=-1
    )


def attend(query_rows, key_rows, value_rows):
    qlen = query_rows.shape[1]
    total = key_rows.shape[1]
    scores = jnp.einsum(
        "bqkgd,bskd->bkgqs", query_rows, key_rows, preferred_element_type=jnp.float32
    ) / jnp.sqrt(jnp.float32(query_rows.shape[-1]))
    key_pos = jnp.arange(total)
    query_pos = jnp.arange(qlen) + (total - qlen)
    allowed = key_pos[None, :] <= query_pos[:, None]
    scores = jnp.where(allowed, scores, -jnp.inf)
    highest = jnp.max(scores, axis=-1, keepdims=True)
    raised = jnp.exp(scores - highest)
    probs = (raised / jnp.sum(raised, axis=-1, keepdims=True)).astype(jnp.bfloat16)
    result = jnp.einsum("bkgqs,bskd->bqkgd", probs, value_rows, preferred_element_type=jnp.float32)
    return result.astype(jnp.bfloat16)


def general(queries, question_kv, pages, page_scales, passage_ids):
    shards = lax.axis_size("store")
    groups_axis = lax.axis_size("head")
    requests, per_request = passage_ids.shape
    fetches = requests * per_request
    stored, part_tokens, lanes = pages.shape
    passage_len = part_tokens * groups_axis
    kv_local = KVH // groups_axis
    groups = QH // KVH
    head_dim = HD
    question_len = queries.shape[0] // requests
    flat_ids = passage_ids.reshape(fetches)
    shard_of = flat_ids // stored
    within = flat_ids % stored
    counter = jnp.arange(fetches)
    same_shard = shard_of[:, None] == shard_of[None, :]
    earlier = counter[None, :] < counter[:, None]
    order_rank = jnp.sum(same_shard & earlier, axis=1)
    slot_index = shard_of * CAP + order_rank
    matches = slot_index[:, None] == jnp.arange(shards * CAP)[None, :]
    wanted_table = jnp.sum(jnp.where(matches, within[:, None], 0), axis=0).reshape(shards, CAP)
    asked = lax.all_to_all(wanted_table, "store", split_axis=0, concat_axis=0, tiled=True)
    asked_flat = asked.reshape(shards * CAP)
    send_pages = jnp.take(pages, asked_flat, axis=0).reshape(shards, CAP, part_tokens, lanes)
    send_scales = jnp.take(page_scales, asked_flat, axis=0).reshape(
        shards, CAP, part_tokens, 2 * KVH
    )
    got_pages, got_scales = (
        lax.all_to_all(
            lax.all_to_all(send_pages, "store", split_axis=0, concat_axis=0, tiled=True),
            "head",
            split_axis=3,
            concat_axis=2,
            tiled=True,
        ),
        lax.all_to_all(
            lax.all_to_all(send_scales, "store", split_axis=0, concat_axis=0, tiled=True),
            "head",
            split_axis=3,
            concat_axis=2,
            tiled=True,
        ),
    )
    mine_pages = jnp.take(
        got_pages.reshape(shards * CAP, passage_len, 2 * kv_local * head_dim), slot_index, axis=0
    )
    mine_scales = jnp.take(
        got_scales.reshape(shards * CAP, passage_len, 2 * kv_local), slot_index, axis=0
    )
    mine_pages = mine_pages.reshape(requests, per_request, passage_len, kv_local, 2, head_dim)
    mine_scales = mine_scales.reshape(requests, per_request, passage_len, kv_local, 2)
    plain = mine_pages.astype(jnp.float32) * mine_scales.astype(jnp.float32)[..., None]
    offsets = jnp.arange(per_request, dtype=jnp.float32) * passage_len
    key_part = (
        rotate_keys(plain[..., 0, :], offsets)
        .astype(jnp.bfloat16)
        .reshape(requests, per_request * passage_len, kv_local, head_dim)
    )
    value_part = (
        plain[..., 1, :]
        .astype(jnp.bfloat16)
        .reshape(requests, per_request * passage_len, kv_local, head_dim)
    )
    question_rows = question_kv.reshape(requests, question_len, kv_local, 2, head_dim)
    key_rows = jnp.concatenate([key_part, question_rows[:, :, :, 0, :]], axis=1)
    value_rows = jnp.concatenate([value_part, question_rows[:, :, :, 1, :]], axis=1)
    query_rows = queries.reshape(requests, question_len, kv_local, groups, head_dim)

    def one_block(items):
        return attend(items[0], items[1], items[2])

    result = lax.map(
        one_block, (query_rows[:, None], key_rows[:, None], value_rows[:, None])
    )
    return result.reshape(requests * question_len, kv_local * groups * head_dim)


def rope_table():
    half = HD // 2
    freqs = np.exp(
        np.arange(half, dtype=np.float32)
        * np.float32(-2.0 * np.log(np.float32(rope_theta)) / np.float32(HD))
    ).astype(np.float32)
    angles = (np.arange(NPAS, dtype=np.float32) * np.float32(PLEN))[:, None] * freqs[None, :]
    angles = angles.astype(np.float64)
    cosine = np.concatenate([np.cos(angles), np.cos(angles)], axis=1)
    sine = np.concatenate([-np.sin(angles), np.sin(angles)], axis=1)
    return np.stack([cosine, sine] * 4, axis=1).astype(np.float32)


def kernel(
    ids_ref, pages_ref, scales_ref, q_ref, qkv_ref, rope_ref,
    out_ref, flag_ref,
    p0, p1, p2, p3, yk1, yk2, yk3, yv1, yv2, yv3, gk0, gk1, gk2, gk3, gv0, gv1, gv2, gv3, gk4,
    s0, s1, s2, s3, s4, s5, s6, s7, s8, l0, l1, l2, l3, l4, l5, l6, l7, l8,
    idv, ids, mine, rope, scaling, queries, question, keys, values, late, probs, late_probs, sums,
    result,
    y_send, y_recv, x_send, x_recv, z_send, z_recv, i_send, i_recv, in_sem, out_sem,
):
    parts = (p0, p1, p2, p3)
    outward = (None, yk1, yk2, yk3, None, yv1, yv2, yv3, None)
    gathered = (gk0, gk1, gk2, gk3, gv0, gv1, gv2, gv3, gk4)
    outgoing = (s0, s1, s2, s3, s4, s5, s6, s7, s8)
    landed = (l0, l1, l2, l3, l4, l5, l6, l7, l8)
    store, head = lax.axis_index("store"), lax.axis_index("head")
    x, z, core = store // (ZS * CORES), (store // CORES) % ZS, store % CORES
    turn = 1 - 2 * core

    def at(x_, z_, core_):
        return ((x_ + 2 * XS) % XS * ZS + z_ % ZS) * CORES + core_

    def spot(x_, core_):
        return (x_ + 2 * XS) % XS * CORES + core_

    here = spot(x, core)

    barrier = pltpu.get_barrier_semaphore()
    peers = [(store, (head + c) % HEADS) for c in range(1, HEADS)]
    peers += [(at(x + 1, z, core), head), (at(x - 1, z, core), head), (at(x, z, 1 - core), head)]
    peers += [(at(x, z + d, core), head) for d in range(1, ZS)]
    for peer in peers:
        pl.semaphore_signal(barrier, inc=1, device_id=peer, device_id_type=MESH)

    def page_copy(c):
        to = (head + HEADS - c) % HEADS
        lanes = pl.ds(pl.multiple_of(to * PART, PART), PART)
        return pltpu.make_async_copy(pages_ref.at[:, lanes], parts[c], in_sem.at[c])

    scale_copy = pltpu.make_async_copy(scales_ref, scaling, in_sem.at[HEADS + 4])
    scale_copy.start()
    for c in range(HEADS):
        page_copy(c).start()
    rope_copy = pltpu.make_async_copy(rope_ref, rope, in_sem.at[HEADS])
    query_copy = pltpu.make_async_copy(q_ref, queries, in_sem.at[HEADS + 1])
    question_copy = pltpu.make_async_copy(qkv_ref, question, in_sem.at[HEADS + 2])
    rope_copy.start()
    query_copy.start()
    question_copy.start()

    planes, over = [], 0
    lane8 = lax.broadcasted_iota(jnp.int32, (8, 128), 1)
    row8 = lax.broadcasted_iota(jnp.int32, (8, 128), 0)
    tile = jnp.zeros((8, 128), jnp.int32)
    for i in range(FETCH):
        one = ids_ref[i // NPAS, i % NPAS]
        plane = (one // P_DEV // CORES) % ZS
        rank = 0
        for other in planes:
            rank = rank + jnp.where(other == plane, 1, 0)
        planes.append(plane)
        over = jnp.maximum(over, rank)
        mine[i] = plane * SLOTS + jnp.minimum(rank, SLOTS - 1)
        code = one + (i % NPAS) * (XS * ZS * CORES * P_DEV)
        tile = jnp.where((lane8 == rank) & (row8 == plane), code, tile)
    idv[z] = jnp.where(lane8 == FETCH, over, tile)

    def id_copy(step):
        return pltpu.make_async_remote_copy(
            src_ref=idv.at[z], dst_ref=idv.at[z],
            send_sem=i_send.at[step], recv_sem=i_recv.at[step],
            device_id=(at(x, z + step, core), head), device_id_type=MESH,
        )

    def y_copy(n):
        c = n % HEADS
        to = (head + HEADS - c) % HEADS
        return pltpu.make_async_remote_copy(
            src_ref=outward[n], dst_ref=gathered[n].at[here],
            send_sem=y_send.at[n], recv_sem=y_recv.at[n],
            device_id=(store, to), device_id_type=MESH,
        )

    def x_copy(n, kind):
        slot, to = (
            (here, at(x + 1, z, core)),
            (here, at(x - 1, z, core)),
            (spot(x - turn, core), at(x + turn, z, core)),
            (here, at(x, z, 1 - core)),
            (spot(x - 1, core), at(x, z, 1 - core)),
            (spot(x + 1, core), at(x, z, 1 - core)),
            (spot(x + 2, core), at(x, z, 1 - core)),
        )[kind]
        return pltpu.make_async_remote_copy(
            src_ref=gathered[n].at[slot], dst_ref=gathered[n].at[slot],
            send_sem=x_send.at[n, kind], recv_sem=x_recv.at[n, kind],
            device_id=(to, head), device_id_type=MESH,
        )

    def z_copy(n, step):
        return pltpu.make_async_remote_copy(
            src_ref=outgoing[n].at[step], dst_ref=landed[n].at[z],
            send_sem=z_send.at[n, step], recv_sem=z_recv.at[n, step],
            device_id=(at(x, z + step, core), head), device_id_type=MESH,
        )

    lane = lax.broadcasted_iota(jnp.int32, (TOK, 128), 1)
    pick_row = lax.broadcasted_iota(jnp.int32, (P_DEV * 2 * KVH, 128), 0)
    pick_lane = lax.broadcasted_iota(jnp.int32, (P_DEV * 2 * KVH, 128), 1)

    def scales_of(col):
        pick = jnp.where(pick_row == 2 * KVH * pick_lane + col, 1.0, 0.0).astype(jnp.bfloat16)
        return lax.dot_general(
            scaling[...], pick, (((0,), (0,)), ((), ())), preferred_element_type=jnp.float32
        )

    def lay_out(c):
        first = 4 * ((head + HEADS - c) % HEADS)
        scales = [scales_of(first + j) for j in range(4)]

        def put_keys(p, rows):
            if c == 0:
                gk0[here, p] = rows[:FIRST].astype(jnp.bfloat16)
                gk4[here, p] = rows[FIRST:].astype(jnp.bfloat16)
            else:
                outward[c][p] = rows.astype(jnp.bfloat16)

        def put_values(p, rows):
            if c == 0:
                gv0[here, p] = rows.astype(jnp.bfloat16)
            else:
                outward[HEADS + c][p] = rows.astype(jnp.bfloat16)

        put_keys(P_DEV, jnp.concatenate([scales[0], scales[2]], axis=0))

        def two_pages(i, carry):
            pair = pl.ds(pl.multiple_of(i * ROWS, ROWS), ROWS)
            codes = [
                parts[c][pair, LANES * g : LANES * (g + 1)].astype(jnp.float32) for g in range(2)
            ]
            for half in range(2):
                p, rows = 2 * i + half, slice(half * TOK, (half + 1) * TOK)
                value_half = []
                for g in range(2):
                    scale = jnp.sum(
                        jnp.where(lane == p, scales[2 * g + 1], 0.0), axis=1, keepdims=True
                    )
                    value_half.append(codes[g][rows, HD:] * scale)
                put_keys(p, jnp.concatenate([codes[g][rows, :HD] for g in range(2)], axis=0))
                put_values(p, jnp.concatenate(value_half, axis=0))
            return carry

        lax.fori_loop(0, P_DEV // 2, two_pages, 0)

    def x_start(n):
        if n % HEADS > 0:
            y_copy(n).wait_recv()
        if n == HEADS - 1:
            gk3[here, P_DEV, :, HD // 2 :] = jnp.broadcast_to(flag, (ROWS, HD // 2)).astype(
                jnp.bfloat16
            )
        for kind in (0, 1, 3):
            x_copy(n, kind).start()

    def x_forward(n):
        x_copy(n, 0).wait_recv()
        x_copy(n, 1).wait_recv()
        for kind in (2, 4, 5):
            x_copy(n, kind).start()

    def x_last(n):
        x_copy(n, 2).wait_recv()
        x_copy(n, 6).start()

    def x_done(n):
        for kind in (3, 4, 5, 6):
            x_copy(n, kind).wait_recv()

    def finished(n, code):
        slot = code % P_DEV
        shard = (code // P_DEV) % (XS * ZS * CORES)
        k = code // (XS * ZS * CORES * P_DEV)
        place = (shard // (ZS * CORES)) * CORES + shard % CORES
        block = gathered[n][place, slot]
        if not holds_keys(n):
            return block
        rows_lane = lax.broadcasted_iota(jnp.int32, (rows_of(n), 128), 1)
        scales = gathered[n][place, P_DEV].astype(jnp.float32)
        scale = jnp.sum(jnp.where(rows_lane == slot, scales, 0.0), axis=1, keepdims=True)
        key = block.astype(jnp.float32) * scale
        turned = key * rope[k, 0:1] + pltpu.roll(key, HD // 2, 1) * rope[k, 1:2]
        return turned.astype(jnp.bfloat16)

    def z_start(n):
        def one_dest(i, carry):
            step = (i * 3) % ZS
            to = (z + step) % ZS
            for j in range(SLOTS):
                outgoing[n][step, j] = finished(n, ids[to, z, j])
            z_copy(n, step).start()
            return carry

        lax.fori_loop(1, ZS, one_dest, 0)
        for j in range(SLOTS):
            landed[n][z, j] = finished(n, ids[z, z, j])

    scale_copy.wait()
    page_copy(0).wait()
    lay_out(0)
    pl.semaphore_wait(barrier, len(peers))
    for step in range(1, ZS):
        id_copy(step).start()
    x_start(ORDER[0])
    x_start(ORDER[1])
    for c in (1, 3):
        page_copy(c).wait()
        lay_out(c)
        y_copy(c).start()
    x_forward(ORDER[0])
    page_copy(2).wait()
    lay_out(2)
    y_copy(2).start()
    rope_copy.wait()

    for step in range(1, ZS):
        id_copy(step).wait_recv()
    to_smem = pltpu.make_async_copy(idv, ids, in_sem.at[HEADS + 3])
    to_smem.start()
    to_smem.wait()

    worst = ids[0, 0, FETCH]
    for dest in range(1, ZS):
        worst = jnp.maximum(worst, ids[dest, 0, FETCH])
    flag = jnp.where(worst >= SLOTS, 1.0, 0.0)

    x_start(ORDER[2])
    x_last(0)
    x_forward(ORDER[1])
    x_done(0)
    z_start(0)
    for n in ORDER[6:]:
        y_copy(n).start()
    for i in range(1, CHUNKS):
        x_last(ORDER[i])
        if i + 1 < CHUNKS:
            x_forward(ORDER[i + 1])
        if i + 2 < CHUNKS:
            x_start(ORDER[i + 2])
        x_done(ORDER[i])
        z_start(ORDER[i])

    flags = gk3[0, P_DEV].astype(jnp.float32)
    for place in range(1, SHARDS):
        flags = jnp.maximum(flags, gk3[place, P_DEV].astype(jnp.float32))
    flag_ref[0, 0] = jnp.max(flags[:8, HD // 2 :]).astype(jnp.int32)

    def arrived(n):
        def one(step, carry):
            z_copy(n, step).wait_recv()
            return carry

        lax.fori_loop(1, ZS, one, 0)

    def passages(ns, r):
        blocks = []
        for k in range(NPAS):
            place = mine[r * NPAS + k]
            pieces = [landed[n][place // SLOTS, place % SLOTS].astype(jnp.float32) for n in ns]
            blocks.append(pieces[0] if len(ns) == 1 else jnp.concatenate(pieces, axis=0))
        return [
            jnp.concatenate([b[g * TOK : (g + 1) * TOK] for b in blocks], axis=0).astype(
                jnp.bfloat16
            )
            for g in range(2)
        ]

    early = [c for c in (0, 1, 3, 2) if c != LAST]
    for n in [n for n in ORDER if holds_keys(n)]:
        arrived(n)
    query_copy.wait()
    question_copy.wait()

    col = lax.broadcasted_iota(jnp.int32, (GROUPS * QLEN, QLEN), 1)
    row = lax.broadcasted_iota(jnp.int32, (GROUPS * QLEN, QLEN), 0) % QLEN
    seen = col <= row

    def weigh(r, carry):
        rows = pl.ds(pl.multiple_of(r * QLEN, QLEN), QLEN)
        for i, c in enumerate(early + [LAST]):
            for g, part in enumerate(passages((0, REST) if c == 0 else (c,), r)):
                keys[g, i * PIECE : (i + 1) * PIECE, :] = part
        for g in range(2):
            keys[g, PKEYS:, :] = question[rows, g * LANES : g * LANES + HD]
            values[r, g, PKEYS - PIECE :, :] = question[rows, g * LANES + HD : (g + 1) * LANES]
            query = jnp.concatenate(
                [
                    queries[rows, (g * GROUPS + j) * HD : (g * GROUPS + j + 1) * HD]
                    for j in range(GROUPS)
                ],
                axis=0,
            )
            dims = (((1,), (1,)), ((), ()))
            scale = jnp.float32(1.0 / math.sqrt(HD))
            past = scale * lax.dot_general(
                query, keys[g, :PKEYS, :], dims, preferred_element_type=jnp.float32
            )
            now = scale * lax.dot_general(
                query, keys[g, PKEYS:, :], dims, preferred_element_type=jnp.float32
            )
            now = jnp.where(seen, now, -jnp.inf)
            top = jnp.maximum(
                jnp.max(past, axis=1, keepdims=True), jnp.max(now, axis=1, keepdims=True)
            )
            past = jnp.exp(past - top)
            now = jnp.exp(now - top)
            total = jnp.sum(past, axis=1, keepdims=True) + jnp.sum(now, axis=1, keepdims=True)
            inverse = 1.0 / total
            past = (past * inverse).astype(jnp.bfloat16)
            probs[r, g, :, : PKEYS - PIECE] = past[:, : PKEYS - PIECE]
            probs[r, g, :, PKEYS - PIECE :] = (now * inverse).astype(jnp.bfloat16)
            late_probs[r, g] = past[:, PKEYS - PIECE :]
        return carry

    lax.fori_loop(0, R_DEV, weigh, 0)

    for i, c in enumerate(early):
        arrived(HEADS + c)

        def place_values(r, carry, i=i, c=c):
            for g, part in enumerate(passages((HEADS + c,), r)):
                values[r, g, i * PIECE : (i + 1) * PIECE, :] = part
            return carry

        lax.fori_loop(0, R_DEV, place_values, 0)

    def mix_early(r, carry):
        for g in range(2):
            sums[r, g] = jnp.dot(probs[r, g], values[r, g], preferred_element_type=jnp.float32)
        return carry

    lax.fori_loop(0, R_DEV, mix_early, 0)
    arrived(HEADS + LAST)

    def out_copy(r):
        rows = pl.ds(pl.multiple_of(r * QLEN, QLEN), QLEN)
        return pltpu.make_async_copy(result.at[r], out_ref.at[rows], out_sem.at[r])

    def mix(r, carry):
        for g, part in enumerate(passages((HEADS + LAST,), r)):
            late[g] = part
        for g in range(2):
            mixed = sums[r, g] + jnp.dot(
                late_probs[r, g], late[g], preferred_element_type=jnp.float32
            )
            for j in range(GROUPS):
                result[r, :, (g * GROUPS + j) * HD : (g * GROUPS + j + 1) * HD] = mixed[
                    j * QLEN : (j + 1) * QLEN
                ].astype(jnp.bfloat16)
        out_copy(r).start()
        return carry

    lax.fori_loop(0, R_DEV, mix, 0)

    for step in range(1, ZS):
        id_copy(step).wait_send()
    for n in range(CHUNKS):
        if n % HEADS > 0:
            y_copy(n).wait_send()
        for kind in range(7):
            x_copy(n, kind).wait_send()
        for step in range(1, ZS):
            z_copy(n, step).wait_send()
    for r in range(R_DEV):
        out_copy(r).wait()


def fast(queries, question_kv, pages, page_scales, passage_ids):
    smem = pl.BlockSpec(memory_space=pltpu.SMEM)
    hbm = pl.BlockSpec(memory_space=pl.ANY)
    block = (ROWS, HD)
    dma, bf16 = pltpu.SemaphoreType.DMA, jnp.bfloat16
    rows = pages.reshape(P_DEV * TOK, 2 * KVH * HD)
    scales = page_scales.transpose(0, 2, 1).reshape(P_DEV * 2 * KVH, TOK)
    return pl.pallas_call(
        kernel,
        out_shape=(
            jax.ShapeDtypeStruct(queries.shape, bf16),
            jax.ShapeDtypeStruct((1, 1), jnp.int32),
        ),
        in_specs=[smem] + [hbm] * 5,
        out_specs=(hbm, smem),
        scratch_shapes=[pltpu.VMEM((P_DEV * TOK, PART), bf16)] * HEADS
        + [pltpu.VMEM((P_DEV + 1,) + block, bf16)] * (HEADS - 1)
        + [pltpu.VMEM((P_DEV,) + block, bf16)] * (HEADS - 1)
        + [
            pltpu.VMEM((SHARDS, P_DEV + holds_keys(n), rows_of(n), HD), bf16)
            for n in range(CHUNKS)
        ]
        + [pltpu.VMEM((ZS, SLOTS, rows_of(n), HD), bf16) for n in range(CHUNKS)] * 2
        + [
            pltpu.VMEM((ZS, 8, 128), jnp.int32),
            pltpu.SMEM((ZS, 8, 128), jnp.int32),
            pltpu.SMEM((FETCH,), jnp.int32),
            pltpu.VMEM((NPAS, 8, HD), jnp.float32),
            pltpu.VMEM(scales.shape, bf16),
            pltpu.VMEM(queries.shape, bf16),
            pltpu.VMEM(question_kv.shape, bf16),
            pltpu.VMEM((2, KEYS, HD), bf16),
            pltpu.VMEM((R_DEV, 2, KEYS - PIECE, HD), bf16),
            pltpu.VMEM((2, PIECE, HD), bf16),
            pltpu.VMEM((R_DEV, 2, GROUPS * QLEN, KEYS - PIECE), bf16),
            pltpu.VMEM((R_DEV, 2, GROUPS * QLEN, PIECE), bf16),
            pltpu.VMEM((R_DEV, 2, GROUPS * QLEN, HD), jnp.float32),
            pltpu.VMEM((R_DEV, QLEN, QH // HEADS * HD), bf16),
            dma((CHUNKS,)), dma((CHUNKS,)),
            dma((CHUNKS, 7)), dma((CHUNKS, 7)),
            dma((CHUNKS, ZS)), dma((CHUNKS, ZS)),
            dma((ZS,)), dma((ZS,)),
            dma((HEADS + 5,)), dma((R_DEV,)),
        ],
        compiler_params=pltpu.CompilerParams(
            collective_id=0, has_side_effects=True, vmem_limit_bytes=58 * 1024 * 1024
        ),
    )(passage_ids, rows, scales, queries, question_kv, jnp.asarray(rope_table()))


def per_device(queries, question_kv, pages, page_scales, passage_ids):
    args = (queries, question_kv, pages, page_scales, passage_ids)
    result, flag = fast(*args)
    full = flag[0, 0] > 0
    return lax.cond(full, lambda: general(*args), lambda: result)


def solution(mesh):
    return jax.shard_map(
        per_device,
        mesh=mesh,
        in_specs=(
            P("store", "head"),
            P("store", "head"),
            P("store", "head", None),
            P("store", "head", None),
            P("store", None),
        ),
        out_specs=P("store", "head"),
        check_vma=False,
    )
```

```python
import math

import numpy as np
import jax
import jax.numpy as jnp
from jax import lax
from jax.experimental import pallas as pl
from jax.experimental.pallas import tpu as pltpu
from jax.sharding import PartitionSpec as P

QH = 64
KVH = 8
HD = 128
NPAS = 4
PLEN = 96
CAP = 2
QLEN = 64
R_DEV = 4
P_DEV = 16
XS, ZS, CORES, HEADS = 4, 8, 2, 4
SHARDS = XS * CORES
TOK = PLEN // HEADS
ROWS = 2 * TOK
LANES = 2 * HD
SLOTS = 4
FETCH = R_DEV * NPAS
GROUPS = QH // KVH
PART = 4 * HD
PIECE = NPAS * TOK
PKEYS = NPAS * PLEN
KEYS = PKEYS + QLEN
CHUNKS = 2 * HEADS + 1
REST = CHUNKS - 1
FIRST = 16
ORDER = (0, REST, 4, 1, 3, 2, 5, 7, 6)
LAST = ORDER[-1] - HEADS
MESH = pl.DeviceIdType.MESH

rope_theta = 500000.0


def rows_of(n):
    return FIRST if n == 0 else ROWS - FIRST if n == REST else ROWS


def holds_keys(n):
    return n < HEADS or n == REST


def rotate_keys(keys, offsets):
    half_dim = keys.shape[-1] // 2
    freqs = jnp.exp(
        jnp.arange(half_dim, dtype=jnp.float32)
        * (-2.0 * jnp.log(jnp.float32(rope_theta)) / keys.shape[-1])
    )
    angles = offsets[:, None] * freqs[None, :]
    cosine = jnp.cos(angles)[:, None, None, :]
    sine = jnp.sin(angles)[:, None, None, :]
    first = keys[..., :half_dim]
    second = keys[..., half_dim:]
    return jnp.concatenate(
        [first * cosine - second * sine, second * cosine + first * sine], axis=-1
    )


def attend(query_rows, key_rows, value_rows):
    qlen = query_rows.shape[1]
    total = key_rows.shape[1]
    scores = jnp.einsum(
        "bqkgd,bskd->bkgqs", query_rows, key_rows, preferred_element_type=jnp.float32
    ) / jnp.sqrt(jnp.float32(query_rows.shape[-1]))
    key_pos = jnp.arange(total)
    query_pos = jnp.arange(qlen) + (total - qlen)
    allowed = key_pos[None, :] <= query_pos[:, None]
    scores = jnp.where(allowed, scores, -jnp.inf)
    highest = jnp.max(scores, axis=-1, keepdims=True)
    raised = jnp.exp(scores - highest)
    probs = (raised / jnp.sum(raised, axis=-1, keepdims=True)).astype(jnp.bfloat16)
    result = jnp.einsum("bkgqs,bskd->bqkgd", probs, value_rows, preferred_element_type=jnp.float32)
    return result.astype(jnp.bfloat16)


def general(queries, question_kv, pages, page_scales, passage_ids):
    shards = lax.axis_size("store")
    groups_axis = lax.axis_size("head")
    requests, per_request = passage_ids.shape
    fetches = requests * per_request
    stored, part_tokens, lanes = pages.shape
    passage_len = part_tokens * groups_axis
    kv_local = KVH // groups_axis
    groups = QH // KVH
    head_dim = HD
    question_len = queries.shape[0] // requests
    flat_ids = passage_ids.reshape(fetches)
    shard_of = flat_ids // stored
    within = flat_ids % stored
    counter = jnp.arange(fetches)
    same_shard = shard_of[:, None] == shard_of[None, :]
    earlier = counter[None, :] < counter[:, None]
    order_rank = jnp.sum(same_shard & earlier, axis=1)
    slot_index = shard_of * CAP + order_rank
    matches = slot_index[:, None] == jnp.arange(shards * CAP)[None, :]
    wanted_table = jnp.sum(jnp.where(matches, within[:, None], 0), axis=0).reshape(shards, CAP)
    asked = lax.all_to_all(wanted_table, "store", split_axis=0, concat_axis=0, tiled=True)
    asked_flat = asked.reshape(shards * CAP)
    send_pages = jnp.take(pages, asked_flat, axis=0).reshape(shards, CAP, part_tokens, lanes)
    send_scales = jnp.take(page_scales, asked_flat, axis=0).reshape(
        shards, CAP, part_tokens, 2 * KVH
    )
    got_pages, got_scales = (
        lax.all_to_all(
            lax.all_to_all(send_pages, "store", split_axis=0, concat_axis=0, tiled=True),
            "head",
            split_axis=3,
            concat_axis=2,
            tiled=True,
        ),
        lax.all_to_all(
            lax.all_to_all(send_scales, "store", split_axis=0, concat_axis=0, tiled=True),
            "head",
            split_axis=3,
            concat_axis=2,
            tiled=True,
        ),
    )
    mine_pages = jnp.take(
        got_pages.reshape(shards * CAP, passage_len, 2 * kv_local * head_dim), slot_index, axis=0
    )
    mine_scales = jnp.take(
        got_scales.reshape(shards * CAP, passage_len, 2 * kv_local), slot_index, axis=0
    )
    mine_pages = mine_pages.reshape(requests, per_request, passage_len, kv_local, 2, head_dim)
    mine_scales = mine_scales.reshape(requests, per_request, passage_len, kv_local, 2)
    plain = mine_pages.astype(jnp.float32) * mine_scales.astype(jnp.float32)[..., None]
    offsets = jnp.arange(per_request, dtype=jnp.float32) * passage_len
    key_part = (
        rotate_keys(plain[..., 0, :], offsets)
        .astype(jnp.bfloat16)
        .reshape(requests, per_request * passage_len, kv_local, head_dim)
    )
    value_part = (
        plain[..., 1, :]
        .astype(jnp.bfloat16)
        .reshape(requests, per_request * passage_len, kv_local, head_dim)
    )
    question_rows = question_kv.reshape(requests, question_len, kv_local, 2, head_dim)
    key_rows = jnp.concatenate([key_part, question_rows[:, :, :, 0, :]], axis=1)
    value_rows = jnp.concatenate([value_part, question_rows[:, :, :, 1, :]], axis=1)
    query_rows = queries.reshape(requests, question_len, kv_local, groups, head_dim)

    def one_block(items):
        return attend(items[0], items[1], items[2])

    result = lax.map(
        one_block, (query_rows[:, None], key_rows[:, None], value_rows[:, None])
    )
    return result.reshape(requests * question_len, kv_local * groups * head_dim)


def rope_table():
    half = HD // 2
    freqs = np.exp(
        np.arange(half, dtype=np.float32)
        * np.float32(-2.0 * np.log(np.float32(rope_theta)) / np.float32(HD))
    ).astype(np.float32)
    angles = (np.arange(NPAS, dtype=np.float32) * np.float32(PLEN))[:, None] * freqs[None, :]
    angles = angles.astype(np.float64)
    cosine = np.concatenate([np.cos(angles), np.cos(angles)], axis=1)
    sine = np.concatenate([-np.sin(angles), np.sin(angles)], axis=1)
    return np.stack([cosine, sine] * 4, axis=1).astype(np.float32)


def kernel(
    ids_ref, pages_ref, scales_ref, q_ref, qkv_ref, rope_ref,
    out_ref, flag_ref,
    p0, p1, p2, p3, yk1, yk2, yk3, yv1, yv2, yv3, gk0, gk1, gk2, gk3, gv0, gv1, gv2, gv3, gk4,
    s0, s1, s2, s3, s4, s5, s6, s7, s8, l0, l1, l2, l3, l4, l5, l6, l7, l8,
    idv, ids, mine, rope, scaling, queries, question, keys, values, late, probs, late_probs, sums,
    result,
    y_send, y_recv, x_send, x_recv, z_send, z_recv, i_send, i_recv, in_sem, out_sem,
):
    parts = (p0, p1, p2, p3)
    outward = (None, yk1, yk2, yk3, None, yv1, yv2, yv3, None)
    gathered = (gk0, gk1, gk2, gk3, gv0, gv1, gv2, gv3, gk4)
    outgoing = (s0, s1, s2, s3, s4, s5, s6, s7, s8)
    landed = (l0, l1, l2, l3, l4, l5, l6, l7, l8)
    store, head = lax.axis_index("store"), lax.axis_index("head")
    x, z, core = store // (ZS * CORES), (store // CORES) % ZS, store % CORES
    turn = 1 - 2 * core

    def at(x_, z_, core_):
        return ((x_ + 2 * XS) % XS * ZS + z_ % ZS) * CORES + core_

    def spot(x_, core_):
        return (x_ + 2 * XS) % XS * CORES + core_

    here = spot(x, core)

    barrier = pltpu.get_barrier_semaphore()
    peers = [(store, (head + c) % HEADS) for c in range(1, HEADS)]
    peers += [(at(x + 1, z, core), head), (at(x - 1, z, core), head), (at(x, z, 1 - core), head)]
    peers += [(at(x, z + d, core), head) for d in range(1, ZS)]
    for peer in peers:
        pl.semaphore_signal(barrier, inc=1, device_id=peer, device_id_type=MESH)

    def page_copy(c):
        to = (head + HEADS - c) % HEADS
        lanes = pl.ds(pl.multiple_of(to * PART, PART), PART)
        return pltpu.make_async_copy(pages_ref.at[:, lanes], parts[c], in_sem.at[c])

    scale_copy = pltpu.make_async_copy(scales_ref, scaling, in_sem.at[HEADS + 4])
    scale_copy.start()
    for c in range(HEADS):
        page_copy(c).start()
    rope_copy = pltpu.make_async_copy(rope_ref, rope, in_sem.at[HEADS])
    query_copy = pltpu.make_async_copy(q_ref, queries, in_sem.at[HEADS + 1])
    question_copy = pltpu.make_async_copy(qkv_ref, question, in_sem.at[HEADS + 2])
    rope_copy.start()
    query_copy.start()
    question_copy.start()

    planes, over = [], 0
    lane8 = lax.broadcasted_iota(jnp.int32, (8, 128), 1)
    row8 = lax.broadcasted_iota(jnp.int32, (8, 128), 0)
    tile = jnp.zeros((8, 128), jnp.int32)
    for i in range(FETCH):
        one = ids_ref[i // NPAS, i % NPAS]
        plane = (one // P_DEV // CORES) % ZS
        rank = 0
        for other in planes:
            rank = rank + jnp.where(other == plane, 1, 0)
        planes.append(plane)
        over = jnp.maximum(over, rank)
        mine[i] = plane * SLOTS + jnp.minimum(rank, SLOTS - 1)
        code = one + (i % NPAS) * (XS * ZS * CORES * P_DEV)
        tile = jnp.where((lane8 == rank) & (row8 == plane), code, tile)
    idv[z] = jnp.where(lane8 == FETCH, over, tile)

    def id_copy(step):
        return pltpu.make_async_remote_copy(
            src_ref=idv.at[z], dst_ref=idv.at[z],
            send_sem=i_send.at[step], recv_sem=i_recv.at[step],
            device_id=(at(x, z + step, core), head), device_id_type=MESH,
        )

    def y_copy(n):
        c = n % HEADS
        to = (head + HEADS - c) % HEADS
        return pltpu.make_async_remote_copy(
            src_ref=outward[n], dst_ref=gathered[n].at[here],
            send_sem=y_send.at[n], recv_sem=y_recv.at[n],
            device_id=(store, to), device_id_type=MESH,
        )

    def pieces(n):
        blocks = P_DEV + holds_keys(n)
        if n in (0, REST):
            return ((n, pl.ds(0, blocks)),)
        return (n, pl.ds(0, P_DEV // 2)), (CHUNKS + n, pl.ds(P_DEV // 2, blocks - P_DEV // 2))

    def x_copy(n, kind, piece):
        slot, to = (
            (here, at(x + 1, z, core)),
            (here, at(x - 1, z, core)),
            (spot(x - turn, core), at(x + turn, z, core)),
            (here, at(x, z, 1 - core)),
            (spot(x - 1, core), at(x, z, 1 - core)),
            (spot(x + 1, core), at(x, z, 1 - core)),
            (spot(x + 2, core), at(x, z, 1 - core)),
        )[kind]
        return pltpu.make_async_remote_copy(
            src_ref=gathered[n].at[slot, piece[1]], dst_ref=gathered[n].at[slot, piece[1]],
            send_sem=x_send.at[piece[0], kind], recv_sem=x_recv.at[piece[0], kind],
            device_id=(to, head), device_id_type=MESH,
        )

    def z_copy(n, step):
        return pltpu.make_async_remote_copy(
            src_ref=outgoing[n].at[step], dst_ref=landed[n].at[z],
            send_sem=z_send.at[n, step], recv_sem=z_recv.at[n, step],
            device_id=(at(x, z + step, core), head), device_id_type=MESH,
        )

    lane = lax.broadcasted_iota(jnp.int32, (TOK, 128), 1)
    pick_row = lax.broadcasted_iota(jnp.int32, (P_DEV * 2 * KVH, 128), 0)
    pick_lane = lax.broadcasted_iota(jnp.int32, (P_DEV * 2 * KVH, 128), 1)

    def scales_of(col):
        pick = jnp.where(pick_row == 2 * KVH * pick_lane + col, 1.0, 0.0).astype(jnp.bfloat16)
        return lax.dot_general(
            scaling[...], pick, (((0,), (0,)), ((), ())), preferred_element_type=jnp.float32
        )

    def lay_out(c):
        first = 4 * ((head + HEADS - c) % HEADS)
        scales = [scales_of(first + j) for j in range(4)]

        def put_keys(p, rows):
            if c == 0:
                gk0[here, p] = rows[:FIRST].astype(jnp.bfloat16)
                gk4[here, p] = rows[FIRST:].astype(jnp.bfloat16)
            else:
                outward[c][p] = rows.astype(jnp.bfloat16)

        def put_values(p, rows):
            if c == 0:
                gv0[here, p] = rows.astype(jnp.bfloat16)
            else:
                outward[HEADS + c][p] = rows.astype(jnp.bfloat16)

        put_keys(P_DEV, jnp.concatenate([scales[0], scales[2]], axis=0))

        def two_pages(i, carry):
            pair = pl.ds(pl.multiple_of(i * ROWS, ROWS), ROWS)
            codes = [
                parts[c][pair, LANES * g : LANES * (g + 1)].astype(jnp.float32) for g in range(2)
            ]
            for half in range(2):
                p, rows = 2 * i + half, slice(half * TOK, (half + 1) * TOK)
                value_half = []
                for g in range(2):
                    scale = jnp.sum(
                        jnp.where(lane == p, scales[2 * g + 1], 0.0), axis=1, keepdims=True
                    )
                    value_half.append(codes[g][rows, HD:] * scale)
                put_keys(p, jnp.concatenate([codes[g][rows, :HD] for g in range(2)], axis=0))
                put_values(p, jnp.concatenate(value_half, axis=0))
            return carry

        lax.fori_loop(0, P_DEV // 2, two_pages, 0)

    def x_start(n):
        if n % HEADS > 0:
            y_copy(n).wait_recv()
        if n == HEADS - 1:
            gk3[here, P_DEV, :, HD // 2 :] = jnp.broadcast_to(flag, (ROWS, HD // 2)).astype(
                jnp.bfloat16
            )
        for piece in pieces(n):
            for kind in (0, 1, 3):
                x_copy(n, kind, piece).start()

    def x_forward(n):
        for piece in pieces(n):
            x_copy(n, 0, piece).wait_recv()
            x_copy(n, 1, piece).wait_recv()
            for kind in (2, 4, 5):
                x_copy(n, kind, piece).start()

    def x_last(n):
        for piece in pieces(n):
            x_copy(n, 2, piece).wait_recv()
            x_copy(n, 6, piece).start()

    def x_done(n):
        for piece in pieces(n):
            for kind in (3, 4, 5, 6):
                x_copy(n, kind, piece).wait_recv()

    def finished(n, code):
        slot = code % P_DEV
        shard = (code // P_DEV) % (XS * ZS * CORES)
        k = code // (XS * ZS * CORES * P_DEV)
        place = (shard // (ZS * CORES)) * CORES + shard % CORES
        block = gathered[n][place, slot]
        if not holds_keys(n):
            return block
        rows_lane = lax.broadcasted_iota(jnp.int32, (rows_of(n), 128), 1)
        scales = gathered[n][place, P_DEV].astype(jnp.float32)
        scale = jnp.sum(jnp.where(rows_lane == slot, scales, 0.0), axis=1, keepdims=True)
        key = block.astype(jnp.float32) * scale
        turned = key * rope[k, 0:1] + pltpu.roll(key, HD // 2, 1) * rope[k, 1:2]
        return turned.astype(jnp.bfloat16)

    def z_start(n):
        def one_dest(i, carry):
            step = (i * 3) % ZS
            to = (z + step) % ZS
            for j in range(SLOTS):
                outgoing[n][step, j] = finished(n, ids[to, z, j])
            z_copy(n, step).start()
            return carry

        lax.fori_loop(1, ZS, one_dest, 0)
        for j in range(SLOTS):
            landed[n][z, j] = finished(n, ids[z, z, j])

    scale_copy.wait()
    page_copy(0).wait()
    lay_out(0)
    pl.semaphore_wait(barrier, len(peers))
    for step in range(1, ZS):
        id_copy(step).start()
    x_start(ORDER[0])
    x_start(ORDER[1])
    for c in (1, 3):
        page_copy(c).wait()
        lay_out(c)
        y_copy(c).start()
    x_forward(ORDER[0])
    page_copy(2).wait()
    lay_out(2)
    y_copy(2).start()
    rope_copy.wait()

    for step in range(1, ZS):
        id_copy(step).wait_recv()
    to_smem = pltpu.make_async_copy(idv, ids, in_sem.at[HEADS + 3])
    to_smem.start()
    to_smem.wait()

    worst = ids[0, 0, FETCH]
    for dest in range(1, ZS):
        worst = jnp.maximum(worst, ids[dest, 0, FETCH])
    flag = jnp.where(worst >= SLOTS, 1.0, 0.0)

    x_start(ORDER[2])
    x_last(0)
    x_forward(ORDER[1])
    x_done(0)
    z_start(0)
    for n in ORDER[6:]:
        y_copy(n).start()
    for i in range(1, CHUNKS):
        x_last(ORDER[i])
        if i + 1 < CHUNKS:
            x_forward(ORDER[i + 1])
        if i + 2 < CHUNKS:
            x_start(ORDER[i + 2])
        x_done(ORDER[i])
        z_start(ORDER[i])

    flags = gk3[0, P_DEV].astype(jnp.float32)
    for place in range(1, SHARDS):
        flags = jnp.maximum(flags, gk3[place, P_DEV].astype(jnp.float32))
    flag_ref[0, 0] = jnp.max(flags[:8, HD // 2 :]).astype(jnp.int32)

    def arrived(n):
        def one(step, carry):
            z_copy(n, step).wait_recv()
            return carry

        lax.fori_loop(1, ZS, one, 0)

    def passages(ns, r):
        blocks = []
        for k in range(NPAS):
            place = mine[r * NPAS + k]
            pieces = [landed[n][place // SLOTS, place % SLOTS].astype(jnp.float32) for n in ns]
            blocks.append(pieces[0] if len(ns) == 1 else jnp.concatenate(pieces, axis=0))
        return [
            jnp.concatenate([b[g * TOK : (g + 1) * TOK] for b in blocks], axis=0).astype(
                jnp.bfloat16
            )
            for g in range(2)
        ]

    early = [c for c in (0, 1, 3, 2) if c != LAST]
    for n in [n for n in ORDER if holds_keys(n)]:
        arrived(n)
    query_copy.wait()
    question_copy.wait()

    col = lax.broadcasted_iota(jnp.int32, (GROUPS * QLEN, QLEN), 1)
    row = lax.broadcasted_iota(jnp.int32, (GROUPS * QLEN, QLEN), 0) % QLEN
    seen = col <= row

    def weigh(r, carry):
        rows = pl.ds(pl.multiple_of(r * QLEN, QLEN), QLEN)
        for i, c in enumerate(early + [LAST]):
            for g, part in enumerate(passages((0, REST) if c == 0 else (c,), r)):
                keys[g, i * PIECE : (i + 1) * PIECE, :] = part
        for g in range(2):
            keys[g, PKEYS:, :] = question[rows, g * LANES : g * LANES + HD]
            values[r, g, PKEYS - PIECE :, :] = question[rows, g * LANES + HD : (g + 1) * LANES]
            query = jnp.concatenate(
                [
                    queries[rows, (g * GROUPS + j) * HD : (g * GROUPS + j + 1) * HD]
                    for j in range(GROUPS)
                ],
                axis=0,
            )
            dims = (((1,), (1,)), ((), ()))
            scale = jnp.float32(1.0 / math.sqrt(HD))
            past = scale * lax.dot_general(
                query, keys[g, :PKEYS, :], dims, preferred_element_type=jnp.float32
            )
            now = scale * lax.dot_general(
                query, keys[g, PKEYS:, :], dims, preferred_element_type=jnp.float32
            )
            now = jnp.where(seen, now, -jnp.inf)
            top = jnp.maximum(
                jnp.max(past, axis=1, keepdims=True), jnp.max(now, axis=1, keepdims=True)
            )
            past = jnp.exp(past - top)
            now = jnp.exp(now - top)
            total = jnp.sum(past, axis=1, keepdims=True) + jnp.sum(now, axis=1, keepdims=True)
            inverse = 1.0 / total
            past = (past * inverse).astype(jnp.bfloat16)
            probs[r, g, :, : PKEYS - PIECE] = past[:, : PKEYS - PIECE]
            probs[r, g, :, PKEYS - PIECE :] = (now * inverse).astype(jnp.bfloat16)
            late_probs[r, g] = past[:, PKEYS - PIECE :]
        return carry

    lax.fori_loop(0, R_DEV, weigh, 0)

    for i, c in enumerate(early):
        arrived(HEADS + c)

        def place_values(r, carry, i=i, c=c):
            for g, part in enumerate(passages((HEADS + c,), r)):
                values[r, g, i * PIECE : (i + 1) * PIECE, :] = part
            return carry

        lax.fori_loop(0, R_DEV, place_values, 0)

    def mix_early(r, carry):
        for g in range(2):
            sums[r, g] = jnp.dot(probs[r, g], values[r, g], preferred_element_type=jnp.float32)
        return carry

    lax.fori_loop(0, R_DEV, mix_early, 0)
    arrived(HEADS + LAST)

    def out_copy(r):
        rows = pl.ds(pl.multiple_of(r * QLEN, QLEN), QLEN)
        return pltpu.make_async_copy(result.at[r], out_ref.at[rows], out_sem.at[r])

    def mix(r, carry):
        for g, part in enumerate(passages((HEADS + LAST,), r)):
            late[g] = part
        for g in range(2):
            mixed = sums[r, g] + jnp.dot(
                late_probs[r, g], late[g], preferred_element_type=jnp.float32
            )
            for j in range(GROUPS):
                result[r, :, (g * GROUPS + j) * HD : (g * GROUPS + j + 1) * HD] = mixed[
                    j * QLEN : (j + 1) * QLEN
                ].astype(jnp.bfloat16)
        out_copy(r).start()
        return carry

    lax.fori_loop(0, R_DEV, mix, 0, unroll=True)

    for step in range(1, ZS):
        id_copy(step).wait_send()
    for n in range(CHUNKS):
        if n % HEADS > 0:
            y_copy(n).wait_send()
        for piece in pieces(n):
            for kind in range(7):
                x_copy(n, kind, piece).wait_send()
        for step in range(1, ZS):
            z_copy(n, step).wait_send()
    for r in range(R_DEV):
        out_copy(r).wait()


def fast(queries, question_kv, pages, page_scales, passage_ids):
    smem = pl.BlockSpec(memory_space=pltpu.SMEM)
    hbm = pl.BlockSpec(memory_space=pl.ANY)
    block = (ROWS, HD)
    dma, bf16 = pltpu.SemaphoreType.DMA, jnp.bfloat16
    rows = pages.reshape(P_DEV * TOK, 2 * KVH * HD)
    scales = page_scales.transpose(0, 2, 1).reshape(P_DEV * 2 * KVH, TOK)
    return pl.pallas_call(
        kernel,
        out_shape=(
            jax.ShapeDtypeStruct(queries.shape, bf16),
            jax.ShapeDtypeStruct((1, 1), jnp.int32),
        ),
        in_specs=[smem] + [hbm] * 5,
        out_specs=(hbm, smem),
        scratch_shapes=[pltpu.VMEM((P_DEV * TOK, PART), bf16)] * HEADS
        + [pltpu.VMEM((P_DEV + 1,) + block, bf16)] * (HEADS - 1)
        + [pltpu.VMEM((P_DEV,) + block, bf16)] * (HEADS - 1)
        + [
            pltpu.VMEM((SHARDS, P_DEV + holds_keys(n), rows_of(n), HD), bf16)
            for n in range(CHUNKS)
        ]
        + [pltpu.VMEM((ZS, SLOTS, rows_of(n), HD), bf16) for n in range(CHUNKS)] * 2
        + [
            pltpu.VMEM((ZS, 8, 128), jnp.int32),
            pltpu.SMEM((ZS, 8, 128), jnp.int32),
            pltpu.SMEM((FETCH,), jnp.int32),
            pltpu.VMEM((NPAS, 8, HD), jnp.float32),
            pltpu.VMEM(scales.shape, bf16),
            pltpu.VMEM(queries.shape, bf16),
            pltpu.VMEM(question_kv.shape, bf16),
            pltpu.VMEM((2, KEYS, HD), bf16),
            pltpu.VMEM((R_DEV, 2, KEYS - PIECE, HD), bf16),
            pltpu.VMEM((2, PIECE, HD), bf16),
            pltpu.VMEM((R_DEV, 2, GROUPS * QLEN, KEYS - PIECE), bf16),
            pltpu.VMEM((R_DEV, 2, GROUPS * QLEN, PIECE), bf16),
            pltpu.VMEM((R_DEV, 2, GROUPS * QLEN, HD), jnp.float32),
            pltpu.VMEM((R_DEV, QLEN, QH // HEADS * HD), bf16),
            dma((CHUNKS,)), dma((CHUNKS,)),
            dma((2 * CHUNKS, 7)), dma((2 * CHUNKS, 7)),
            dma((CHUNKS, ZS)), dma((CHUNKS, ZS)),
            dma((ZS,)), dma((ZS,)),
            dma((HEADS + 5,)), dma((R_DEV,)),
        ],
        compiler_params=pltpu.CompilerParams(
            collective_id=0, has_side_effects=True, vmem_limit_bytes=58 * 1024 * 1024
        ),
    )(passage_ids, rows, scales, queries, question_kv, jnp.asarray(rope_table()))


def per_device(queries, question_kv, pages, page_scales, passage_ids):
    args = (queries, question_kv, pages, page_scales, passage_ids)
    result, flag = fast(*args)
    full = flag[0, 0] > 0
    return lax.cond(full, lambda: general(*args), lambda: result)


def solution(mesh):
    return jax.shard_map(
        per_device,
        mesh=mesh,
        in_specs=(
            P("store", "head"),
            P("store", "head"),
            P("store", "head", None),
            P("store", "head", None),
            P("store", None),
        ),
        out_specs=P("store", "head"),
        check_vma=False,
    )
```
